128 devices in a mesh: vdp: 32 (over y, z, core), seq: 4 (over x).
Axes of the slice: x: 4, y: 4, z: 4, core: 2. Of those that a mesh axis runs over, the one named last changes fastest.
Arguments:
- pre_act: bfloat16 [8192, 5120], P(('vdp', 'seq')), may hold values from -6 to 6
- proj_weight: bfloat16 [5120, 8192], P('vdp', 'seq'), may hold values from -0.078125 to 0.078125
- proj_bias: bfloat16 [8192], P('seq'), may hold values from -3 to 3
- frame_tokens: int32 [32, 32], replicated, may hold values from 6 to 8, as said below
- frame_sample: int32 [32, 32], replicated, may hold values from 0 to 31, as said below
- clip_offset: int32 [32, 32], replicated, may hold values from 0 to 506, as said below
- embed_grad: bfloat16 [16384, 8192], P(('vdp', 'seq')), may hold values from -6 to 6
Outputs:
- image_embeds: bfloat16 [16384, 8192], P(('vdp', 'seq'))
- pre_grad: bfloat16 [8192, 5120], P(('vdp', 'seq'))
The draws below stay inside these ranges and needn't reach their ends.
Inputs may be any that keep to these rules, and one draw needn't show every extreme that they name: `frame_tokens`: in every draw at least one vision group has all its frames at 8 merged tokens; the frames of other groups hold 6 to 8. `frame_sample`: each vision group sends exactly 1 of its frames to each sequence. The frames of group g with frame_sample equal to t, in frame order, occupy positions clip_offset[g, t] onward of sequence t; within a sequence these runs don't intersect and end by position 512. In every draw a run of 8 tokens begins at the first position of its sequence.
All inputs are finite; a program needn't handle non-finite values.
Results may differ from the reference program's by a relative error of at most 0.015.
Values may be sent and summed in bfloat16 or wider, within the bound.
No kernel may reach another device: no remote copies, remote signals or barrier semaphores. Data moves between devices by JAX's collectives and lax.ppermute only.
A program may use at most 128 MiB of HBM per device.

```python
import jax
import jax.numpy as jnp
from jax import lax

D = 8192
HID = 5120
FRAMES = 32
MAXTOK = 8
ROWS = 256
LEN = 512
N_VDP = 32
N_SEQ = 4


def frame_layout(key):
    key_tokens, key_full, key_assign, key_order, key_gaps, key_first = jax.random.split(key, 6)
    group_count = N_VDP
    group_ids = jnp.arange(group_count, dtype=jnp.int32)
    tokens = jax.random.randint(key_tokens, (group_count, FRAMES), MAXTOK - 2, MAXTOK + 1).astype(jnp.int32)
    full_group = jax.random.randint(key_full, (), 0, group_count)
    tokens = jnp.where(group_ids[:, None] == full_group, MAXTOK, tokens).astype(jnp.int32)
    cycle = jnp.arange(FRAMES, dtype=jnp.int32) % group_count
    assign_keys = jax.random.split(key_assign, group_count)
    frame_sample = jax.vmap(lambda sub_key: jax.random.permutation(sub_key, cycle))(assign_keys).astype(jnp.int32)
    matches = frame_sample[:, :, None] == group_ids[None, None, :]
    clip_len = jnp.sum(jnp.where(matches, tokens[:, :, None], 0), axis=1).astype(jnp.int32)
    order_keys = jax.random.split(key_order, group_count)
    seats = jax.vmap(lambda sub_key: jax.random.permutation(sub_key, group_ids))(order_keys).astype(jnp.int32)
    first_sample = jax.random.randint(key_first, (), 0, group_count)
    lead_seat = seats[first_sample, full_group]
    rotated = (seats - lead_seat) % group_count
    seats = jnp.where(group_ids[:, None] == first_sample, rotated, seats).astype(jnp.int32)
    weights = jax.random.randint(key_gaps, (group_count, group_count + 1), 1, 5).astype(jnp.int32)
    gap_ids = jnp.arange(group_count + 1, dtype=jnp.int32)
    weights = jnp.where((group_ids[:, None] == first_sample) & (gap_ids[None, :] == 0), 0, weights).astype(jnp.int32)
    clip_by_sample = clip_len.T
    earlier = seats[:, None, :] < seats[:, :, None]
    preceding = jnp.sum(jnp.where(earlier, clip_by_sample[:, None, :], 0), axis=2).astype(jnp.int32)
    spare = (LEN - jnp.sum(clip_by_sample, axis=1)).astype(jnp.int32)
    cumulative = jnp.cumsum(weights, axis=1).astype(jnp.int32)
    reach = jnp.take_along_axis(cumulative, seats, axis=1)
    offsets = preceding + spare[:, None] * reach // cumulative[:, -1:]
    return (tokens, frame_sample, offsets.T.astype(jnp.int32))


def draw_frame_tokens(key, part):
    shared = frame_layout(key)
    return shared[0]


def draw_frame_sample(key, part):
    shared = frame_layout(key)
    return shared[1]


def draw_clip_offset(key, part):
    shared = frame_layout(key)
    return shared[2]


def level_of(own_key, extent, pieces, smallest, top_value):
    factor_of = 1.0
    for position, shards_of in pieces:
        steps = jax.random.uniform(jax.random.fold_in(jax.random.fold_in(own_key, 6), position), (shards_of,), jnp.float32, smallest / len(pieces), top_value / len(pieces))
        factor_of = factor_of * jnp.repeat(jnp.exp(steps), extent[position] // shards_of).reshape((-1,) + (1,) * (len(extent) - 1 - position))
    return factor_of


def noise(rng, dims, width, limit, shards=(), held_as=jnp.bfloat16):
    values = jax.random.normal(rng, dims, jnp.float32) * width
    if len(shards) > 0:
        values = level_of(rng, dims, shards, -0.22, 0.18) * values
    return jnp.clip(values, min=-limit, max=limit).astype(held_as)


def setup_inputs(seed: int = 0) -> dict:
    key_of = jax.random.split(jax.random.key(seed), 8)
    return {
        "pre_act": noise(key_of[0], (N_VDP * ROWS, HID), 1.0, 6.0, ((0, 128),)),
        "proj_weight": noise(key_of[1], (HID, D), HID ** -0.5, 0.078125, ((0, 32), (1, 4))),
        "proj_bias": noise(key_of[2], (D,), 0.5, 3.0, ((0, 4),)),
        "frame_tokens": draw_frame_tokens(jax.random.fold_in(key_of[7], 71), 0),
        "frame_sample": draw_frame_sample(jax.random.fold_in(key_of[7], 71), 0),
        "clip_offset": draw_clip_offset(jax.random.fold_in(key_of[7], 71), 0),
        "embed_grad": noise(key_of[6], (N_VDP * LEN, D), 1.0, 6.0, ((0, 128),)),
    }


def gelu_exact(values):
    return 0.5 * values * (1.0 + jax.scipy.special.erf(values * 0.7071067811865476))


def gelu_slope(values):
    normal_cdf = 0.5 * (1.0 + jax.scipy.special.erf(values * 0.7071067811865476))
    return normal_cdf + values * jnp.exp(-0.5 * values * values) * 0.3989422804014327


def row_layout(frame_tokens, frame_sample, clip_offset, total_rows):
    frames = frame_tokens.shape[1]
    frame_ends = jnp.cumsum(frame_tokens, axis=1).astype(jnp.int32)
    frame_starts = (frame_ends - frame_tokens).astype(jnp.int32)
    frame_ids = jnp.arange(frames, dtype=jnp.int32)
    same_clip = frame_sample[:, :, None] == frame_sample[:, None, :]
    earlier = frame_ids[None, :] < frame_ids[:, None]
    preceding = jnp.sum(jnp.where(same_clip & earlier[None], frame_tokens[:, None, :], 0), axis=2).astype(jnp.int32)
    frame_position = (jnp.take_along_axis(clip_offset, frame_sample, axis=1) + preceding).astype(jnp.int32)
    row_ids = jnp.arange(total_rows, dtype=jnp.int32)
    frame_of_row = jnp.sum((row_ids[None, :, None] >= frame_starts[:, None, :]).astype(jnp.int32), axis=2).astype(jnp.int32) - 1
    is_live = row_ids[None, :] < frame_ends[:, -1:]
    frame_safe = jnp.clip(frame_of_row, 0, frames - 1).astype(jnp.int32)
    row_start = jnp.take_along_axis(frame_starts, frame_safe, axis=1)
    samples = jnp.take_along_axis(frame_sample, frame_safe, axis=1).astype(jnp.int32)
    positions = (jnp.take_along_axis(frame_position, frame_safe, axis=1) + row_ids[None, :] - row_start).astype(jnp.int32)
    clip_starts = jnp.take_along_axis(clip_offset, samples, axis=1).astype(jnp.int32)
    return samples, positions, clip_starts, is_live


def reference(pre_act, proj_weight, proj_bias, frame_tokens, frame_sample, clip_offset, embed_grad):
    group_count = N_VDP
    samples, positions, clip_starts, is_live = row_layout(frame_tokens, frame_sample, clip_offset, ROWS)
    target_row = jnp.where(is_live, samples * LEN + positions, group_count * LEN).astype(jnp.int32)
    group_rows = pre_act.reshape(group_count, ROWS, HID)
    bias_row = proj_bias.astype(jnp.float32)

    def forward(buffer, inputs):
        block_rows, targets = inputs
        activated = gelu_exact(block_rows.astype(jnp.float32)).astype(jnp.bfloat16)
        projected = (jnp.dot(activated, proj_weight, preferred_element_type=jnp.float32) + bias_row).astype(jnp.bfloat16)
        return buffer.at[targets].set(projected), None

    initial = jnp.zeros((group_count * LEN + 1, D), jnp.bfloat16)
    filled, _ = lax.scan(forward, initial, (group_rows, target_row))
    image_embeds = filled[:group_count * LEN]

    padded = jnp.concatenate([embed_grad, jnp.zeros((1, D), embed_grad.dtype)], axis=0)
    slab_width = D // N_SEQ

    def backward(inputs):
        block_rows, targets = inputs
        row_grad = padded[targets]
        summed = jnp.zeros((ROWS, HID), jnp.float32)
        for quarter in range(N_SEQ):
            grad_cols = row_grad[:, quarter * slab_width:(quarter + 1) * slab_width]
            weight_cols = proj_weight[:, quarter * slab_width:(quarter + 1) * slab_width]
            partial_value = lax.dot_general(grad_cols, weight_cols, (((1,), (1,)), ((), ())), preferred_element_type=jnp.float32)
            summed = summed + lax.optimization_barrier(partial_value.astype(jnp.bfloat16)).astype(jnp.float32)
        return (summed * gelu_slope(block_rows.astype(jnp.float32))).astype(jnp.bfloat16)

    pre_grad = lax.map(backward, (group_rows, target_row)).reshape(group_count * ROWS, HID)
    return image_embeds, pre_grad
```

```python
import jax
import jax.numpy as jnp
from jax import lax
from jax.sharding import PartitionSpec as P

MAXTOK = 8
CHUNKS = 2


def normal_cdf(values):
    return 0.5 * (1.0 + jax.scipy.special.erf(values * 0.7071067811865476))


def one_hot(condition):
    return condition.astype(jnp.bfloat16)


def pick(selector, table):
    return jnp.dot(selector, table, preferred_element_type=jnp.float32).astype(jnp.bfloat16)


def pick_t(selector, table):
    return lax.dot_general(
        selector, table, (((0,), (0,)), ((), ())), preferred_element_type=jnp.float32
    ).astype(jnp.bfloat16)


def slot_of_rows(frame_tokens, frame_sample, own_group, total_rows, slot_total):
    frames = frame_tokens.shape[1]
    tokens = lax.dynamic_slice_in_dim(frame_tokens, own_group, 1, 0)
    sample = lax.dynamic_slice_in_dim(frame_sample, own_group, 1, 0)
    frame_ids = jnp.arange(frames, dtype=jnp.int32)
    before = frame_ids[None, :] < frame_ids[:, None]
    starts = jnp.sum(jnp.where(before, tokens, 0), axis=1)[None, :]
    slots = lax.broadcasted_iota(jnp.int32, (slot_total, frames), 0)
    hit = sample == slots // MAXTOK
    step = (slots % MAXTOK)[:, :1]
    start = jnp.sum(jnp.where(hit, starts, 0), axis=1, keepdims=True)
    length = jnp.sum(jnp.where(hit, tokens, 0), axis=1, keepdims=True)
    row = jnp.where(step < length, start + step, -1)
    return one_hot(row == lax.broadcasted_iota(jnp.int32, (slot_total, total_rows), 1))


def spot_of_slots(frame_tokens, frame_sample, clip_offset, own_seq, seq_len, slot_total):
    groups = frame_tokens.shape[0]
    length = jnp.sum(jnp.where(frame_sample == own_seq, frame_tokens, 0), axis=1)[None, :]
    seq_ids = jnp.arange(clip_offset.shape[1], dtype=jnp.int32)
    offset = jnp.sum(jnp.where(seq_ids[None, :] == own_seq, clip_offset, 0), axis=1)[None, :]
    slots = lax.broadcasted_iota(jnp.int32, (slot_total, groups), 0)
    owner = slots // MAXTOK == lax.broadcasted_iota(jnp.int32, (slot_total, groups), 1)
    step = (slots % MAXTOK)[:, 0]
    slot_length = jnp.sum(jnp.where(owner, length, 0), axis=1)
    slot_offset = jnp.sum(jnp.where(owner, offset, 0), axis=1)
    spot = jnp.where(step < slot_length, slot_offset + step, -1)
    return one_hot(lax.broadcasted_iota(jnp.int32, (seq_len, slot_total), 0) == spot[None, :])


def local(pre_act, proj_weight, proj_bias, frame_tokens, frame_sample, clip_offset, embed_grad):
    groups = lax.axis_size("vdp")
    parts = lax.axis_size("seq")
    own = lax.axis_index("vdp")
    own_rows, hidden = pre_act.shape
    total_rows = own_rows * parts
    span = embed_grad.shape[0]
    seq_len = span * parts
    slab = proj_weight.shape[1]
    slot_total = groups * MAXTOK
    width = slab // CHUNKS

    weights = [
        lax.all_gather(proj_weight[:, q * width : (q + 1) * width], "vdp", axis=0, tiled=True)
        for q in range(CHUNKS)
    ]
    grads = embed_grad.reshape(span, parts, slab).transpose(1, 0, 2)
    columns = lax.all_to_all(grads, "seq", split_axis=0, concat_axis=0, tiled=True)

    rows = pre_act.astype(jnp.float32)
    cdf = normal_cdf(rows)
    activated = (rows * cdf).astype(jnp.bfloat16)
    everyone = lax.all_to_all(
        jnp.broadcast_to(activated[None], (parts, own_rows, hidden)),
        "seq",
        split_axis=0,
        concat_axis=0,
        tiled=True,
    ).reshape(total_rows, hidden)

    by_slot = slot_of_rows(frame_tokens, frame_sample, own, total_rows, slot_total)
    by_spot = spot_of_slots(frame_tokens, frame_sample, clip_offset, own, seq_len, slot_total)

    send_box = pick_t(by_spot, columns.reshape(seq_len, slab)).reshape(groups, MAXTOK, slab)
    returned = lax.all_to_all(send_box, "vdp", split_axis=0, concat_axis=0, tiled=True)
    row_grad = pick_t(by_slot, returned.reshape(slot_total, slab))
    act_slots = pick(by_slot, everyone)

    partial = jnp.zeros((total_rows, hidden), jnp.float32)
    pieces = []
    for q in range(CHUNKS):
        cols = slice(q * width, (q + 1) * width)
        product = jnp.dot(act_slots, weights[q], preferred_element_type=jnp.float32)
        projected = (product + proj_bias[cols].astype(jnp.float32)).astype(jnp.bfloat16)
        incoming = lax.all_to_all(
            projected.reshape(groups, MAXTOK, width), "vdp", split_axis=0, concat_axis=0, tiled=True
        )
        line = pick(by_spot, incoming.reshape(slot_total, width)).reshape(parts, span, width)
        pieces.append(lax.all_to_all(line, "seq", split_axis=0, concat_axis=0, tiled=True))
        partial = partial + lax.dot_general(
            row_grad[:, cols],
            weights[q],
            (((1,), (1,)), ((), ())),
            preferred_element_type=jnp.float32,
        )
    image_embeds = jnp.stack(pieces, axis=2).transpose(1, 0, 2, 3).reshape(span, parts * slab)
    summed = lax.psum_scatter(
        partial.astype(jnp.bfloat16), "seq", scatter_dimension=0, tiled=True
    ).astype(jnp.float32)
    slope = cdf + rows * jnp.exp(-0.5 * rows * rows) * 0.3989422804014327
    pre_grad = (summed * slope).astype(jnp.bfloat16)
    return (image_embeds, pre_grad)


def solution(mesh):
    in_specs = (
        P(("vdp", "seq"), None),
        P("vdp", "seq"),
        P("seq"),
        P(),
        P(),
        P(),
        P(("vdp", "seq"), None),
    )
    out_specs = (P(("vdp", "seq"), None), P(("vdp", "seq"), None))
    return jax.shard_map(local, mesh=mesh, in_specs=in_specs, out_specs=out_specs, check_vma=False)
```

```python
import jax
import jax.numpy as jnp
from jax import lax
from jax.sharding import Mesh, PartitionSpec as P

MAXTOK = 8
Y, Z, CORE, X = "y", "z", "core", "seq"
VDP = (Y, Z, CORE)
ALL = (Y, Z, CORE, X)


def normal_cdf(values):
    return 0.5 * (1.0 + jax.scipy.special.erf(values * 0.7071067811865476))


def pick(selector, table):
    return jnp.dot(selector, table, preferred_element_type=jnp.float32).astype(jnp.bfloat16)


def shift(value, axis, by):
    size = lax.axis_size(axis)
    return lax.ppermute(value, axis, [(i, (i + by) % size) for i in range(size)])


def tie(*values):
    return lax.optimization_barrier(values)


def rows_of_slots(frame_tokens, frame_sample, group, slots):
    tokens = lax.dynamic_slice_in_dim(frame_tokens, group, 1, 0)
    sample = lax.dynamic_slice_in_dim(frame_sample, group, 1, 0)
    frame_ids = jnp.arange(frame_tokens.shape[1], dtype=jnp.int32)
    before = frame_ids[None, :] < frame_ids[:, None]
    starts = jnp.sum(jnp.where(before, tokens, 0), axis=1)[None, :]
    hit = sample == slots // MAXTOK
    step = slots[:, 0] % MAXTOK
    start = jnp.sum(jnp.where(hit, starts, 0), axis=1)
    length = jnp.sum(jnp.where(hit, tokens, 0), axis=1)
    return jnp.where(step < length, start + step, -1)


def spots_of_slots(frame_tokens, frame_sample, clip_offset, own_seq, group_of_slot, step):
    length = jnp.sum(jnp.where(frame_sample == own_seq, frame_tokens, 0), axis=1)[None, :]
    seq_ids = jnp.arange(clip_offset.shape[1], dtype=jnp.int32)
    offset = jnp.sum(jnp.where(seq_ids[None, :] == own_seq, clip_offset, 0), axis=1)[None, :]
    group_ids = jnp.arange(frame_tokens.shape[0], dtype=jnp.int32)
    owner = group_of_slot[:, None] == group_ids[None, :]
    slot_length = jnp.sum(jnp.where(owner, length, 0), axis=1)
    slot_offset = jnp.sum(jnp.where(owner, offset, 0), axis=1)
    return jnp.where(step < slot_length, slot_offset + step, -1)


def hot(index, count):
    return (index[:, None] == jnp.arange(count, dtype=jnp.int32)[None, :]).astype(jnp.bfloat16)


def hot_t(index, count):
    return (jnp.arange(count, dtype=jnp.int32)[:, None] == index[None, :]).astype(jnp.bfloat16)


def local(pre_act, proj_weight, proj_bias, frame_tokens, frame_sample, clip_offset, embed_grad):
    ny, nz, nc, nx = (lax.axis_size(a) for a in ALL)
    iy, iz, ic, ix = (lax.axis_index(a) for a in ALL)
    chip = iy * nz + iz
    own = chip * nc + ic
    sibling = chip * nc + 1 - ic
    groups = ny * nz * nc
    own_rows, hidden = pre_act.shape
    total_rows = own_rows * nx
    span = embed_grad.shape[0]
    seq_len = span * nx
    krows, slab = proj_weight.shape
    half = slab // nc
    slot_total = groups * MAXTOK

    kept = lax.dynamic_slice_in_dim(proj_weight, ic * half, half, 1)
    given = lax.dynamic_slice_in_dim(proj_weight, (1 - ic) * half, half, 1)
    taken = shift(given, CORE, 1)

    rows = pre_act.astype(jnp.float32)
    cdf = normal_cdf(rows)
    activated = (rows * cdf).astype(jnp.bfloat16)
    activated, taken = tie(activated, taken)
    act_right = shift(activated, X, 1)
    act_left = shift(activated, X, -1)

    grads = embed_grad.reshape(span, nx, slab).transpose(1, 0, 2)
    columns = lax.all_to_all(grads, X, split_axis=0, concat_axis=0, tiled=True)
    columns = columns.reshape(seq_len, slab)

    first = jnp.where(ic == 0, kept, taken)
    second = jnp.where(ic == 0, taken, kept)

    weight = jnp.zeros((ny, nz, 2, krows, half), jnp.bfloat16)

    def put(weight, piece, y, z, which):
        zero = jnp.int32(0)
        return lax.dynamic_update_slice(
            weight, piece, (y % ny, z % nz, jnp.int32(which), zero, zero)
        )

    za = [first] + [shift(first, Z, d) for d in (1, -1, 2)]
    yb = [second] + [shift(second, Y, d) for d in (1, -1, 2)]
    line_z = jnp.zeros((nz, krows, half), jnp.bfloat16)
    line_y = jnp.zeros((ny, krows, half), jnp.bfloat16)
    for piece, d in zip(za, (0, 1, -1, 2)):
        line_z = lax.dynamic_update_slice(line_z, piece[None], ((iz - d) % nz, 0, 0))
    for piece, d in zip(yb, (0, 1, -1, 2)):
        line_y = lax.dynamic_update_slice(line_y, piece[None], ((iy - d) % ny, 0, 0))

    act_opp = jnp.concatenate(
        [
            shift(act_right[: own_rows // 2], X, 1),
            shift(act_left[own_rows // 2 :], X, -1),
        ]
    )
    everyone = jnp.zeros((nx, own_rows, hidden), jnp.bfloat16)
    for piece, d in ((activated, 0), (act_right, 1), (act_left, -1), (act_opp, 2)):
        everyone = lax.dynamic_update_slice(everyone, piece[None], ((ix - d) % nx, 0, 0))
    everyone = everyone.reshape(total_rows, hidden)

    zy = [shift(line_z, Y, d) for d in (1, -1)]
    yz = [shift(line_y, Z, d) for d in (1, -1)]

    step = jnp.arange(slot_total, dtype=jnp.int32) % MAXTOK
    pair = jnp.arange(slot_total, dtype=jnp.int32) // (nc * MAXTOK)
    member = jnp.arange(slot_total, dtype=jnp.int32) // MAXTOK % nc
    spot_of = [
        spots_of_slots(
            frame_tokens, frame_sample, clip_offset, own, pair * nc + (member if c == 0 else 1 - member), step
        )
        for c in range(nc)
    ]
    n_slots = nc * slot_total
    ids = lax.broadcasted_iota(jnp.int32, (n_slots, groups), 0)
    slots = ids // (nc * MAXTOK) * MAXTOK + ids % MAXTOK
    from_own = ids[:, 0] // MAXTOK % nc == 0
    row_own = rows_of_slots(frame_tokens, frame_sample, own, slots)
    row_sib = rows_of_slots(frame_tokens, frame_sample, sibling, slots)
    row_of = jnp.where(from_own, row_own, jnp.where(row_sib >= 0, row_sib + total_rows, -1))

    send_box = jnp.stack(
        [
            pick(hot(spot_of[c], seq_len), columns[:, c * half : (c + 1) * half]).reshape(
                ny * nz, nc * MAXTOK, half
            )
            for c in range(nc)
        ],
        axis=1,
    ).reshape(groups, nc * MAXTOK, half)
    returned = lax.all_to_all(send_box, VDP, split_axis=0, concat_axis=0, tiled=True)
    row_grad = pick(hot_t(row_of, nc * total_rows), returned.reshape(n_slots, half))

    other = shift(everyone, CORE, 1)
    act_slots = pick(hot(row_of, nc * total_rows), jnp.concatenate([everyone, other]))

    z_far = [shift(zy[0][: nz // 2], Y, 1), shift(zy[1][nz // 2 :], Y, -1)]
    y_far = [shift(yz[0][: ny // 2], Z, 1), shift(yz[1][ny // 2 :], Z, -1)]
    zero = jnp.int32(0)
    weight = put(weight, line_z[None, :, None], iy, zero, 0)
    weight = put(weight, zy[0][None, :, None], iy - 1, zero, 0)
    weight = put(weight, zy[1][None, :, None], iy + 1, zero, 0)
    weight = put(weight, z_far[0][None, :, None], iy + 2, zero, 0)
    weight = put(weight, z_far[1][None, :, None], iy + 2, zero + nz // 2, 0)
    weight = put(weight, line_y[:, None, None], zero, iz, 1)
    weight = put(weight, yz[0][:, None, None], zero, iz - 1, 1)
    weight = put(weight, yz[1][:, None, None], zero, iz + 1, 1)
    weight = put(weight, y_far[0][:, None, None], zero, iz + 2, 1)
    weight = put(weight, y_far[1][:, None, None], zero + ny // 2, iz + 2, 1)
    weight = weight.reshape(hidden, half)

    bias = lax.dynamic_slice_in_dim(proj_bias, ic * half, half, 0).astype(jnp.float32)
    product = jnp.dot(act_slots, weight, preferred_element_type=jnp.float32)
    projected = (product + bias).astype(jnp.bfloat16)
    incoming = lax.all_to_all(
        projected.reshape(groups, nc * MAXTOK, half), VDP, split_axis=0, concat_axis=0, tiled=True
    ).reshape(ny * nz, nc, nc * MAXTOK, half)

    def back(grad):
        return lax.dot_general(
            grad, weight, (((1,), (1,)), ((), ())), preferred_element_type=jnp.float32
        )

    away = back(row_grad[total_rows:]).astype(jnp.bfloat16)
    received = shift(away, CORE, 1)
    partial = (back(row_grad[:total_rows]) + received.astype(jnp.float32)).astype(jnp.bfloat16)
    parts = partial.reshape(nx, own_rows, hidden)

    def part(d):
        return lax.dynamic_index_in_dim(parts, (ix + d) % nx, 0, keepdims=False)

    mid = hidden // 2
    far = part(2)
    far_right = shift(far[:, :mid], X, 1)
    far_left = shift(far[:, mid:], X, -1)
    to_right, to_left = part(1), part(-1)
    to_right = jnp.concatenate(
        [(to_right[:, :mid].astype(jnp.float32) + far_right).astype(jnp.bfloat16), to_right[:, mid:]], 1
    )
    to_left = jnp.concatenate(
        [to_left[:, :mid], (to_left[:, mid:].astype(jnp.float32) + far_left).astype(jnp.bfloat16)], 1
    )
    got_right = shift(to_right, X, 1)
    got_left = shift(to_left, X, -1)
    summed = part(0).astype(jnp.float32) + got_right.astype(jnp.float32) + got_left.astype(jnp.float32)
    slope = cdf + rows * jnp.exp(-0.5 * rows * rows) * 0.3989422804014327
    pre_grad = (summed * slope).astype(jnp.bfloat16)

    line = jnp.stack(
        [
            pick(hot_t(spot_of[c], seq_len), incoming[:, c].reshape(slot_total, half)).reshape(
                nx, span, half
            )
            for c in range(nc)
        ],
        axis=2,
    ).reshape(nx, span, slab)
    placed = lax.all_to_all(line, X, split_axis=0, concat_axis=0, tiled=True)
    image_embeds = placed.transpose(1, 0, 2).reshape(span, nx * slab)
    return (image_embeds, pre_grad)


def solution(mesh):
    fine = Mesh(mesh.devices.reshape(4, 4, 2, 4), ALL)
    in_specs = (P(ALL, None), P(VDP, X), P(X), P(), P(), P(), P(ALL, None))
    out_specs = (P(ALL, None), P(ALL, None))
    return jax.shard_map(local, mesh=fine, in_specs=in_specs, out_specs=out_specs, check_vma=False)
```

```python
import jax
import jax.numpy as jnp
from jax import lax
from jax.experimental import pallas as pl
from jax.experimental.pallas import tpu as pltpu
from jax.sharding import Mesh, PartitionSpec as P

MAXTOK = 8
Y, Z, CORE, X = "y", "z", "core", "seq"
VDP = (Y, Z, CORE)
ALL = (Y, Z, CORE, X)


def normal_cdf(values):
    return 0.5 * (1.0 + jax.scipy.special.erf(values * 0.7071067811865476))


def shift(value, axis, by):
    size = lax.axis_size(axis)
    return lax.ppermute(value, axis, [(i, (i + by) % size) for i in range(size)])


def tie(*values):
    return lax.optimization_barrier(values)


def rows_of_slots(frame_tokens, frame_sample, group, slots):
    tokens = lax.dynamic_slice_in_dim(frame_tokens, group, 1, 0)
    sample = lax.dynamic_slice_in_dim(frame_sample, group, 1, 0)
    frame_ids = jnp.arange(frame_tokens.shape[1], dtype=jnp.int32)
    before = frame_ids[None, :] < frame_ids[:, None]
    starts = jnp.sum(jnp.where(before, tokens, 0), axis=1)[None, :]
    hit = sample == slots // MAXTOK
    step = slots[:, 0] % MAXTOK
    start = jnp.sum(jnp.where(hit, starts, 0), axis=1)
    length = jnp.sum(jnp.where(hit, tokens, 0), axis=1)
    return jnp.where(step < length, start + step, -1)


def spots_of_slots(frame_tokens, frame_sample, clip_offset, own_seq, group_of_slot, step):
    length = jnp.sum(jnp.where(frame_sample == own_seq, frame_tokens, 0), axis=1)[None, :]
    seq_ids = jnp.arange(clip_offset.shape[1], dtype=jnp.int32)
    offset = jnp.sum(jnp.where(seq_ids[None, :] == own_seq, clip_offset, 0), axis=1)[None, :]
    group_ids = jnp.arange(frame_tokens.shape[0], dtype=jnp.int32)
    owner = group_of_slot[:, None] == group_ids[None, :]
    slot_length = jnp.sum(jnp.where(owner, length, 0), axis=1)
    slot_offset = jnp.sum(jnp.where(owner, offset, 0), axis=1)
    return jnp.where(step < slot_length, slot_offset + step, -1)


VMEM_LIMIT = 48 * 1024 * 1024


def kernel_params():
    return pltpu.CompilerParams(vmem_limit_bytes=VMEM_LIMIT)


def cost(flops, moved):
    return pl.CostEstimate(flops=int(flops), bytes_accessed=int(moved), transcendentals=0)


def split_columns(table, parts):
    rows, total = table.shape
    width = total // parts

    def body(in_ref, out_ref):
        out_ref[0] = in_ref[...]

    return pl.pallas_call(
        body,
        grid=(parts,),
        in_specs=[pl.BlockSpec((rows, width), lambda j: (0, j))],
        out_specs=pl.BlockSpec((1, rows, width), lambda j: (j, 0, 0)),
        out_shape=jax.ShapeDtypeStruct((parts, rows, width), table.dtype),
        compiler_params=kernel_params(),
        cost_estimate=cost(0, 4 * rows * total),
        name="split_columns",
    )(table)


def join_columns(table):
    parts, rows, width = table.shape

    def body(in_ref, out_ref):
        out_ref[...] = in_ref[0]

    return pl.pallas_call(
        body,
        grid=(parts,),
        in_specs=[pl.BlockSpec((1, rows, width), lambda j: (j, 0, 0))],
        out_specs=pl.BlockSpec((rows, width), lambda j: (0, j)),
        out_shape=jax.ShapeDtypeStruct((rows, parts * width), table.dtype),
        compiler_params=kernel_params(),
        cost_estimate=cost(0, 4 * rows * parts * width),
        name="join_columns",
    )(table)


def hot_rows(index, count):
    ids = lax.broadcasted_iota(jnp.int32, (index.shape[0], count), 1)
    return jnp.where(index == ids, 1.0, 0.0).astype(jnp.bfloat16)


def hot_columns(index, count):
    ids = lax.broadcasted_iota(jnp.int32, (count, index.shape[1]), 0)
    return jnp.where(index == ids, 1.0, 0.0).astype(jnp.bfloat16)


def exact(selector, table):
    return jnp.dot(selector, table, preferred_element_type=jnp.float32).astype(jnp.bfloat16)


def gather_spots(spots, columns, chips, cores):
    n = spots.shape[1]
    parts, span, slab = columns.shape
    half = slab // cores
    per = n // chips

    def body(spot_ref, table_ref, out_ref):
        table = table_ref[...].reshape(parts * span, half)
        picked = exact(hot_rows(spot_ref[0], parts * span), table)
        out_ref[...] = picked.reshape(chips, 1, per, half)

    return pl.pallas_call(
        body,
        grid=(cores,),
        in_specs=[
            pl.BlockSpec((1, n, 1), lambda c: (c, 0, 0)),
            pl.BlockSpec((parts, span, half), lambda c: (0, 0, c)),
        ],
        out_specs=pl.BlockSpec((chips, 1, per, half), lambda c: (0, c, 0, 0)),
        out_shape=jax.ShapeDtypeStruct((chips, cores, per, half), columns.dtype),
        compiler_params=kernel_params(),
        cost_estimate=cost(2 * n * parts * span * slab, 4 * parts * span * slab),
        name="gather_spots",
    )(spots, columns)


def scatter_spots(spots, incoming, parts, span):
    chips, cores, per, half = incoming.shape
    n = chips * per

    def body(spot_ref, table_ref, out_ref):
        table = table_ref[...].reshape(n, half)
        placed = exact(hot_columns(spot_ref[0], parts * span), table)
        out_ref[...] = placed.reshape(parts, span, half)

    return pl.pallas_call(
        body,
        grid=(cores,),
        in_specs=[
            pl.BlockSpec((1, 1, n), lambda c: (c, 0, 0)),
            pl.BlockSpec((chips, 1, per, half), lambda c: (0, c, 0, 0)),
        ],
        out_specs=pl.BlockSpec((parts, span, half), lambda c: (0, 0, c)),
        out_shape=jax.ShapeDtypeStruct((parts, span, cores * half), incoming.dtype),
        compiler_params=kernel_params(),
        cost_estimate=cost(2 * n * parts * span * cores * half, 4 * parts * span * cores * half),
        name="scatter_spots",
    )(spots, incoming)


def pick_rows(index, own, other, width):
    n = index.shape[0]
    rows, total = own.shape

    def body(index_ref, own_ref, other_ref, out_ref):
        selector = hot_rows(index_ref[...], 2 * rows)
        picked = jnp.dot(selector[:, :rows], own_ref[...], preferred_element_type=jnp.float32)
        picked += jnp.dot(selector[:, rows:], other_ref[...], preferred_element_type=jnp.float32)
        out_ref[...] = picked.astype(jnp.bfloat16)

    return pl.pallas_call(
        body,
        grid=(total // width,),
        in_specs=[
            pl.BlockSpec((n, 1), lambda j: (0, 0)),
            pl.BlockSpec((rows, width), lambda j: (0, j)),
            pl.BlockSpec((rows, width), lambda j: (0, j)),
        ],
        out_specs=pl.BlockSpec((n, width), lambda j: (0, j)),
        out_shape=jax.ShapeDtypeStruct((n, total), own.dtype),
        compiler_params=kernel_params(),
        cost_estimate=cost(4 * n * rows * total, 8 * rows * total),
        name="pick_rows",
    )(index, own, other)


def unpick_rows(index, table, rows):
    n, width = table.shape

    def body(index_ref, table_ref, out_ref):
        out_ref[...] = exact(hot_columns(index_ref[...], rows), table_ref[...])

    return pl.pallas_call(
        body,
        out_shape=jax.ShapeDtypeStruct((rows, width), table.dtype),
        compiler_params=kernel_params(),
        cost_estimate=cost(2 * n * rows * width, 4 * rows * width),
        name="unpick_rows",
    )(index, table)


def project_back(places, grad, pieces, block, hidden):
    n, half = grad.shape
    tile = 1024
    count = len(pieces)
    blocks = [(p, b * block) for p in range(count) for b in range(pieces[p].shape[0] // block)]

    def body(*refs):
        place_ref, grad_ref = refs[:2]
        piece_refs = refs[2 : 2 + count]
        kept_ref, away_ref, weight_ref, held, arrive, leave = refs[2 + count :]
        copies = []
        for i, (p, start) in enumerate(blocks):
            first = pl.multiple_of(place_ref[i], block)
            copies.append(
                pltpu.make_async_copy(
                    piece_refs[p].at[pl.ds(start, block)],
                    held.at[pl.ds(first, block)],
                    arrive.at[i],
                )
            )
        for copy in copies:
            copy.start()
        for copy in copies:
            copy.wait()
        onward = pltpu.make_async_copy(held, weight_ref, leave)
        onward.start()

        @pl.loop(0, hidden // tile)
        def _(j):
            span = pl.ds(pl.multiple_of(j * tile, tile), tile)
            product = lax.dot_general(
                grad_ref[...],
                held[span, :],
                (((1,), (1,)), ((), ())),
                preferred_element_type=jnp.float32,
            )
            kept_ref[:, span] = product[: n // 2].astype(jnp.bfloat16)
            away_ref[:, span] = product[n // 2 :].astype(jnp.bfloat16)

        onward.wait()

    vmem = pl.BlockSpec(memory_space=pltpu.VMEM)
    anywhere = pl.BlockSpec(memory_space=pl.ANY)
    return pl.pallas_call(
        body,
        in_specs=[pl.BlockSpec(memory_space=pltpu.SMEM), vmem] + [anywhere] * count,
        out_specs=[vmem, vmem, anywhere],
        out_shape=[
            jax.ShapeDtypeStruct((n // 2, hidden), jnp.bfloat16),
            jax.ShapeDtypeStruct((n // 2, hidden), jnp.bfloat16),
            jax.ShapeDtypeStruct((hidden, half), jnp.bfloat16),
        ],
        scratch_shapes=[
            pltpu.VMEM((hidden, half), jnp.bfloat16),
            pltpu.SemaphoreType.DMA((len(blocks),)),
            pltpu.SemaphoreType.DMA,
        ],
        compiler_params=kernel_params(),
        cost_estimate=cost(2 * n * hidden * half, 6 * hidden * half),
        name="project_back",
    )(places, grad, *pieces)


def project(act, bias, weight):
    n, k = act.shape
    half = weight.shape[1]
    tile = 512
    last = k // tile - 1

    def body(act_ref, bias_ref, weight_ref, out_ref, total):
        j = pl.program_id(0)
        product = jnp.dot(act_ref[...], weight_ref[...], preferred_element_type=jnp.float32)

        @pl.when(j == 0)
        def _():
            total[...] = product

        @pl.when(j > 0)
        def _():
            total[...] += product

        @pl.when(j == last)
        def _():
            out_ref[...] = (total[...] + bias_ref[...]).astype(jnp.bfloat16)

    return pl.pallas_call(
        body,
        grid=(k // tile,),
        in_specs=[
            pl.BlockSpec((n, tile), lambda j: (0, j)),
            pl.BlockSpec((1, half), lambda j: (0, 0)),
            pl.BlockSpec((tile, half), lambda j: (j, 0)),
        ],
        out_specs=pl.BlockSpec((n, half), lambda j: (0, 0)),
        out_shape=jax.ShapeDtypeStruct((n, half), jnp.bfloat16),
        scratch_shapes=[pltpu.VMEM((n, half), jnp.float32)],
        compiler_params=kernel_params(),
        cost_estimate=cost(2 * n * k * half, 2 * k * half),
        name="project",
    )(act, bias, weight)


def local(pre_act, proj_weight, proj_bias, frame_tokens, frame_sample, clip_offset, embed_grad):
    ny, nz, nc, nx = (lax.axis_size(a) for a in ALL)
    iy, iz, ic, ix = (lax.axis_index(a) for a in ALL)
    chip = iy * nz + iz
    own = chip * nc + ic
    sibling = chip * nc + 1 - ic
    groups = ny * nz * nc
    own_rows, hidden = pre_act.shape
    total_rows = own_rows * nx
    span = embed_grad.shape[0]
    seq_len = span * nx
    krows, slab = proj_weight.shape
    half = slab // nc
    slot_total = groups * MAXTOK

    rows = pre_act.astype(jnp.float32)
    cdf = normal_cdf(rows)
    activated = (rows * cdf).astype(jnp.bfloat16)
    columns = lax.all_to_all(
        split_columns(embed_grad, nx), X, split_axis=0, concat_axis=0, tiled=True
    )

    step = jnp.arange(slot_total, dtype=jnp.int32) % MAXTOK
    pair = jnp.arange(slot_total, dtype=jnp.int32) // (nc * MAXTOK)
    member = jnp.arange(slot_total, dtype=jnp.int32) // MAXTOK % nc
    spots = jnp.stack(
        [
            spots_of_slots(
                frame_tokens, frame_sample, clip_offset, own, pair * nc + (member if c == 0 else 1 - member), step
            )
            for c in range(nc)
        ]
    )
    n_slots = nc * slot_total
    ids = lax.broadcasted_iota(jnp.int32, (n_slots, groups), 0)
    slots = ids // (nc * MAXTOK) * MAXTOK + ids % MAXTOK
    from_own = ids[:, 0] // MAXTOK % nc == 0
    row_own = rows_of_slots(frame_tokens, frame_sample, own, slots)
    row_sib = rows_of_slots(frame_tokens, frame_sample, sibling, slots)
    row_of = jnp.where(from_own, row_own, jnp.where(row_sib >= 0, row_sib + total_rows, -1))
    def cross(value, near, by):
        pairs = []
        for y in range(ny):
            for z in range(nz):
                for c in range(nc):
                    to = (y, (z + by) % nz) if (c == 0) == near else ((y + by) % ny, z)
                    pairs.append(((y * nz + z) * nc + c, (to[0] * nz + to[1]) * nc + c))
        return lax.ppermute(value, VDP, pairs)

    steps = (0, -1, 1, 2)
    line = jnp.concatenate([proj_weight] + [cross(proj_weight, True, d) for d in (1, -1, 2)])
    mine = lax.dynamic_slice_in_dim(line, ic * half, half, 1)
    theirs = shift(lax.dynamic_slice_in_dim(line, (1 - ic) * half, half, 1), CORE, 1)
    lines = list(tie(mine, theirs, columns, activated))
    columns, activated = lines[2:]
    right, left = shift(activated, X, 1), shift(activated, X, -1)
    plus = [cross(lines[0], False, 1), cross(lines[1], True, 1)]
    minus = [cross(lines[0], False, -1), cross(lines[1], True, -1)]
    plus[0], plus[1], minus[0], minus[1] = tie(*plus, *minus)
    middle = 2 * krows
    far = [
        (
            cross(plus[whose][:middle], whose == 1, 1),
            cross(minus[whose][middle:], whose == 1, -1),
        )
        for whose in range(nc)
    ]
    pieces, places = [], []
    for whose in range(nc):
        which = ic if whose == 0 else 1 - ic
        for piece, nears, away_by in (
            (lines[whose], steps, 0),
            (plus[whose], steps, -1),
            (minus[whose], steps, 1),
            (far[whose][0], steps[:2], 2),
            (far[whose][1], steps[2:], 2),
        ):
            pieces.append(piece)
            for near_by in nears:
                dy = jnp.where(which == 0, away_by, near_by)
                dz = jnp.where(which == 0, near_by, away_by)
                places.append((((iy + dy) % ny * nz + (iz + dz) % nz) * nc + which) * krows)
    places = jnp.stack(places).astype(jnp.int32)

    send_box = gather_spots(spots[:, :, None], columns, ny * nz, nc)
    everyone = jnp.concatenate(
        [
            activated,
            right,
            left,
            shift(tie(right, send_box)[0][: own_rows // 2], X, 1),
            shift(tie(left, send_box)[0][own_rows // 2 :], X, -1),
        ]
    )
    away_by = (row_of // own_rows - ix) % nx
    seat = jnp.where(away_by == nx - 1, 1, jnp.where(away_by == 0, 0, away_by + 1))
    act_row = jnp.where(
        row_of < 0, -1, row_of // total_rows * total_rows + seat * own_rows + row_of % own_rows
    )

    returned = lax.all_to_all(
        send_box.reshape(groups, nc * MAXTOK, half), VDP, split_axis=0, concat_axis=0, tiled=True
    )
    returned = tie(returned, *far[0], *far[1])[0]
    row_grad = unpick_rows(row_of[None, :], returned.reshape(n_slots, half), nc * total_rows)

    other = shift(everyone, CORE, 1)
    act_slots = pick_rows(act_row[:, None], everyone, other, hidden // 4)

    bias = lax.dynamic_slice_in_dim(proj_bias, ic * half, half, 0).astype(jnp.float32)[None, :]
    kept_sum, away, weight = project_back(places, row_grad, pieces, krows, hidden)
    received = shift(away, CORE, 1).reshape(nx, own_rows, hidden)
    kept_sum = kept_sum.reshape(nx, own_rows, hidden)
    projected = project(act_slots, bias, weight)
    incoming = lax.all_to_all(
        projected.reshape(groups, nc * MAXTOK, half), VDP, split_axis=0, concat_axis=0, tiled=True
    ).reshape(ny * nz, nc, nc * MAXTOK, half)

    def part(d):
        here = (ix + d) % nx
        mine = lax.dynamic_index_in_dim(kept_sum, here, 0, keepdims=False)
        theirs = lax.dynamic_index_in_dim(received, here, 0, keepdims=False)
        return mine.astype(jnp.float32) + theirs.astype(jnp.float32)

    mid = hidden // 2
    far = part(2).astype(jnp.bfloat16)
    far_right = shift(far[:, :mid], X, 1)
    far_left = shift(far[:, mid:], X, -1)
    to_right, to_left = part(1), part(-1)
    got_right_top = shift((to_right[:, :mid] + far_right.astype(jnp.float32)).astype(jnp.bfloat16), X, 1)
    got_right_end = shift(to_right[:, mid:].astype(jnp.bfloat16), X, 1)
    got_left_top = shift(to_left[:, :mid].astype(jnp.bfloat16), X, -1)
    got_left_end = shift((to_left[:, mid:] + far_left.astype(jnp.float32)).astype(jnp.bfloat16), X, -1)
    arrived = jnp.concatenate(
        [
            got_right_top.astype(jnp.float32) + got_left_top.astype(jnp.float32),
            got_right_end.astype(jnp.float32) + got_left_end.astype(jnp.float32),
        ],
        axis=1,
    )
    summed = part(0) + arrived
    slope = cdf + rows * jnp.exp(-0.5 * rows * rows) * 0.3989422804014327
    pre_grad = (summed * slope).astype(jnp.bfloat16)

    line = scatter_spots(spots[:, None, :], incoming, nx, span)
    placed = lax.all_to_all(line, X, split_axis=0, concat_axis=0, tiled=True)
    placed, pre_grad = tie(placed, pre_grad)
    return (join_columns(placed), pre_grad)


def solution(mesh):
    fine = Mesh(mesh.devices.reshape(4, 4, 2, 4), ALL)
    in_specs = (P(ALL, None), P(VDP, X), P(X), P(), P(), P(), P(ALL, None))
    out_specs = (P(ALL, None), P(ALL, None))
    return jax.shard_map(local, mesh=fine, in_specs=in_specs, out_specs=out_specs, check_vma=False)
```

```python
import jax
import jax.numpy as jnp
from jax import lax
from jax.experimental import pallas as pl
from jax.experimental.pallas import tpu as pltpu
from jax.sharding import Mesh, PartitionSpec as P

MAXTOK = 8
Y, Z, CORE, X = "y", "z", "core", "seq"
VDP = (Y, Z, CORE)
ALL = (Y, Z, CORE, X)


def normal_cdf(values):
    return 0.5 * (1.0 + jax.scipy.special.erf(values * 0.7071067811865476))


def shift(value, axis, by):
    size = lax.axis_size(axis)
    return lax.ppermute(value, axis, [(i, (i + by) % size) for i in range(size)])


def tie(*values):
    return lax.optimization_barrier(values)


def rows_of_slots(frame_tokens, frame_sample, group, slots):
    tokens = lax.dynamic_slice_in_dim(frame_tokens, group, 1, 0)
    sample = lax.dynamic_slice_in_dim(frame_sample, group, 1, 0)
    frame_ids = jnp.arange(frame_tokens.shape[1], dtype=jnp.int32)
    before = frame_ids[None, :] < frame_ids[:, None]
    starts = jnp.sum(jnp.where(before, tokens, 0), axis=1)[None, :]
    hit = sample == slots // MAXTOK
    step = slots[:, 0] % MAXTOK
    start = jnp.sum(jnp.where(hit, starts, 0), axis=1)
    length = jnp.sum(jnp.where(hit, tokens, 0), axis=1)
    return jnp.where(step < length, start + step, -1)


def spots_of_slots(frame_tokens, frame_sample, clip_offset, own_seq, group_of_slot, step):
    length = jnp.sum(jnp.where(frame_sample == own_seq, frame_tokens, 0), axis=1)[None, :]
    seq_ids = jnp.arange(clip_offset.shape[1], dtype=jnp.int32)
    offset = jnp.sum(jnp.where(seq_ids[None, :] == own_seq, clip_offset, 0), axis=1)[None, :]
    group_ids = jnp.arange(frame_tokens.shape[0], dtype=jnp.int32)
    owner = group_of_slot[:, None] == group_ids[None, :]
    slot_length = jnp.sum(jnp.where(owner, length, 0), axis=1)
    slot_offset = jnp.sum(jnp.where(owner, offset, 0), axis=1)
    return jnp.where(step < slot_length, slot_offset + step, -1)


VMEM_LIMIT = 48 * 1024 * 1024


def kernel_params():
    return pltpu.CompilerParams(vmem_limit_bytes=VMEM_LIMIT)


def cost(flops, moved):
    return pl.CostEstimate(flops=int(flops), bytes_accessed=int(moved), transcendentals=0)


def split_columns(table, parts):
    rows, total = table.shape
    width = total // parts

    def body(in_ref, out_ref):
        out_ref[0] = in_ref[...]

    return pl.pallas_call(
        body,
        grid=(parts,),
        in_specs=[pl.BlockSpec((rows, width), lambda j: (0, j))],
        out_specs=pl.BlockSpec((1, rows, width), lambda j: (j, 0, 0)),
        out_shape=jax.ShapeDtypeStruct((parts, rows, width), table.dtype),
        compiler_params=kernel_params(),
        cost_estimate=cost(0, 4 * rows * total),
        name="split_columns",
    )(table)


def join_columns(table):
    parts, rows, width = table.shape

    def body(in_ref, out_ref):
        out_ref[...] = in_ref[0]

    return pl.pallas_call(
        body,
        grid=(parts,),
        in_specs=[pl.BlockSpec((1, rows, width), lambda j: (j, 0, 0))],
        out_specs=pl.BlockSpec((rows, width), lambda j: (0, j)),
        out_shape=jax.ShapeDtypeStruct((rows, parts * width), table.dtype),
        compiler_params=kernel_params(),
        cost_estimate=cost(0, 4 * rows * parts * width),
        name="join_columns",
    )(table)


def hot_rows(index, count):
    ids = lax.broadcasted_iota(jnp.int32, (index.shape[0], count), 1)
    return jnp.where(index == ids, 1.0, 0.0).astype(jnp.bfloat16)


def hot_columns(index, count):
    ids = lax.broadcasted_iota(jnp.int32, (count, index.shape[1]), 0)
    return jnp.where(index == ids, 1.0, 0.0).astype(jnp.bfloat16)


def exact(selector, table):
    return jnp.dot(selector, table, preferred_element_type=jnp.float32).astype(jnp.bfloat16)


def gather_spots(spots, columns, chips, cores):
    n = spots.shape[1]
    parts, span, slab = columns.shape
    half = slab // cores
    per = n // chips

    def body(spot_ref, table_ref, out_ref):
        table = table_ref[...].reshape(parts * span, half)
        picked = exact(hot_rows(spot_ref[0], parts * span), table)
        out_ref[...] = picked.reshape(chips, 1, per, half)

    return pl.pallas_call(
        body,
        grid=(cores,),
        in_specs=[
            pl.BlockSpec((1, n, 1), lambda c: (c, 0, 0)),
            pl.BlockSpec((parts, span, half), lambda c: (0, 0, c)),
        ],
        out_specs=pl.BlockSpec((chips, 1, per, half), lambda c: (0, c, 0, 0)),
        out_shape=jax.ShapeDtypeStruct((chips, cores, per, half), columns.dtype),
        compiler_params=kernel_params(),
        cost_estimate=cost(2 * n * parts * span * slab, 4 * parts * span * slab),
        name="gather_spots",
    )(spots, columns)


def scatter_spots(spots, incoming, parts, span):
    chips, cores, per, half = incoming.shape
    n = chips * per

    def body(spot_ref, table_ref, out_ref):
        table = table_ref[...].reshape(n, half)
        placed = exact(hot_columns(spot_ref[0], parts * span), table)
        out_ref[...] = placed.reshape(parts, span, half)

    return pl.pallas_call(
        body,
        grid=(cores,),
        in_specs=[
            pl.BlockSpec((1, 1, n), lambda c: (c, 0, 0)),
            pl.BlockSpec((chips, 1, per, half), lambda c: (0, c, 0, 0)),
        ],
        out_specs=pl.BlockSpec((parts, span, half), lambda c: (0, 0, c)),
        out_shape=jax.ShapeDtypeStruct((parts, span, cores * half), incoming.dtype),
        compiler_params=kernel_params(),
        cost_estimate=cost(2 * n * parts * span * cores * half, 4 * parts * span * cores * half),
        name="scatter_spots",
    )(spots, incoming)


def pick_rows(index, own, other, width):
    n = index.shape[0]
    rows, total = own.shape

    def body(index_ref, own_ref, other_ref, out_ref):
        selector = hot_rows(index_ref[...], 2 * rows)
        picked = jnp.dot(selector[:, :rows], own_ref[...], preferred_element_type=jnp.float32)
        picked += jnp.dot(selector[:, rows:], other_ref[...], preferred_element_type=jnp.float32)
        out_ref[...] = picked.astype(jnp.bfloat16)

    return pl.pallas_call(
        body,
        grid=(total // width,),
        in_specs=[
            pl.BlockSpec((n, 1), lambda j: (0, 0)),
            pl.BlockSpec((rows, width), lambda j: (0, j)),
            pl.BlockSpec((rows, width), lambda j: (0, j)),
        ],
        out_specs=pl.BlockSpec((n, width), lambda j: (0, j)),
        out_shape=jax.ShapeDtypeStruct((n, total), own.dtype),
        compiler_params=kernel_params(),
        cost_estimate=cost(4 * n * rows * total, 8 * rows * total),
        name="pick_rows",
    )(index, own, other)


def unpick_rows(index, table, rows):
    n, width = table.shape

    def body(index_ref, table_ref, out_ref):
        out_ref[...] = exact(hot_columns(index_ref[...], rows), table_ref[...])

    return pl.pallas_call(
        body,
        out_shape=jax.ShapeDtypeStruct((rows, width), table.dtype),
        compiler_params=kernel_params(),
        cost_estimate=cost(2 * n * rows * width, 4 * rows * width),
        name="unpick_rows",
    )(index, table)


def project_back(places, grad, pieces, block, hidden):
    n, half = grad.shape
    tile = 1024
    count = len(pieces)
    blocks = [(p, b * block) for p in range(count) for b in range(pieces[p].shape[0] // block)]

    def body(*refs):
        place_ref, grad_ref = refs[:2]
        piece_refs = refs[2 : 2 + count]
        kept_ref, away_ref, weight_ref, held, arrive, leave = refs[2 + count :]
        copies = []
        for i, (p, start) in enumerate(blocks):
            first = pl.multiple_of(place_ref[i], block)
            copies.append(
                pltpu.make_async_copy(
                    piece_refs[p].at[pl.ds(start, block)],
                    held.at[pl.ds(first, block)],
                    arrive.at[i],
                )
            )
        for copy in copies:
            copy.start()
        for copy in copies:
            copy.wait()
        onward = pltpu.make_async_copy(held, weight_ref, leave)
        onward.start()

        @pl.loop(0, hidden // tile)
        def _(j):
            span = pl.ds(pl.multiple_of(j * tile, tile), tile)
            product = lax.dot_general(
                grad_ref[...],
                held[span, :],
                (((1,), (1,)), ((), ())),
                preferred_element_type=jnp.float32,
            )
            kept_ref[:, span] = product[: n // 2].astype(jnp.bfloat16)
            away_ref[:, span] = product[n // 2 :].astype(jnp.bfloat16)

        onward.wait()

    vmem = pl.BlockSpec(memory_space=pltpu.VMEM)
    anywhere = pl.BlockSpec(memory_space=pl.ANY)
    return pl.pallas_call(
        body,
        in_specs=[pl.BlockSpec(memory_space=pltpu.SMEM), vmem] + [anywhere] * count,
        out_specs=[vmem, vmem, anywhere],
        out_shape=[
            jax.ShapeDtypeStruct((n // 2, hidden), jnp.bfloat16),
            jax.ShapeDtypeStruct((n // 2, hidden), jnp.bfloat16),
            jax.ShapeDtypeStruct((hidden, half), jnp.bfloat16),
        ],
        scratch_shapes=[
            pltpu.VMEM((hidden, half), jnp.bfloat16),
            pltpu.SemaphoreType.DMA((len(blocks),)),
            pltpu.SemaphoreType.DMA,
        ],
        compiler_params=kernel_params(),
        cost_estimate=cost(2 * n * hidden * half, 6 * hidden * half),
        name="project_back",
    )(places, grad, *pieces)


def project(act, bias, weight, part, parts, earlier):
    n, k = act.shape
    half = weight.shape[1]
    width = half // parts
    tile = 1024
    last = k // tile - 1

    def body(act_ref, bias_ref, weight_ref, *rest):
        out_ref, total = rest[-2:]
        j = pl.program_id(0)
        product = jnp.dot(act_ref[...], weight_ref[...], preferred_element_type=jnp.float32)

        @pl.when(j == 0)
        def _():
            total[...] = product

        @pl.when(j > 0)
        def _():
            total[...] += product

        @pl.when(j == last)
        def _():
            out_ref[...] = (total[...] + bias_ref[...]).astype(jnp.bfloat16)

    return pl.pallas_call(
        body,
        grid=(k // tile,),
        in_specs=[
            pl.BlockSpec((n, tile), lambda j: (0, j)),
            pl.BlockSpec((1, width), lambda j: (0, part)),
            pl.BlockSpec((tile, width), lambda j: (j, part)),
        ]
        + [pl.BlockSpec(memory_space=pl.ANY)] * len(earlier),
        out_specs=pl.BlockSpec((n, width), lambda j: (0, part)),
        out_shape=jax.ShapeDtypeStruct((n, half), jnp.bfloat16),
        scratch_shapes=[pltpu.VMEM((n, width), jnp.float32)],
        compiler_params=kernel_params(),
        cost_estimate=cost(2 * n * k * width, 2 * k * width),
        input_output_aliases={3: 0} if earlier else {},
        name="project",
    )(act, bias, weight, *earlier)


def local(pre_act, proj_weight, proj_bias, frame_tokens, frame_sample, clip_offset, embed_grad):
    ny, nz, nc, nx = (lax.axis_size(a) for a in ALL)
    iy, iz, ic, ix = (lax.axis_index(a) for a in ALL)
    chip = iy * nz + iz
    own = chip * nc + ic
    sibling = chip * nc + 1 - ic
    groups = ny * nz * nc
    own_rows, hidden = pre_act.shape
    total_rows = own_rows * nx
    span = embed_grad.shape[0]
    seq_len = span * nx
    krows, slab = proj_weight.shape
    half = slab // nc
    slot_total = groups * MAXTOK

    rows = pre_act.astype(jnp.float32)
    cdf = normal_cdf(rows)
    activated = (rows * cdf).astype(jnp.bfloat16)
    columns = lax.all_to_all(
        split_columns(embed_grad, nx), X, split_axis=0, concat_axis=0, tiled=True
    )

    step = jnp.arange(slot_total, dtype=jnp.int32) % MAXTOK
    pair = jnp.arange(slot_total, dtype=jnp.int32) // (nc * MAXTOK)
    member = jnp.arange(slot_total, dtype=jnp.int32) // MAXTOK % nc
    spots = jnp.stack(
        [
            spots_of_slots(
                frame_tokens, frame_sample, clip_offset, own, pair * nc + (member if c == 0 else 1 - member), step
            )
            for c in range(nc)
        ]
    )
    n_slots = nc * slot_total
    ids = lax.broadcasted_iota(jnp.int32, (n_slots, groups), 0)
    slots = ids // (nc * MAXTOK) * MAXTOK + ids % MAXTOK
    from_own = ids[:, 0] // MAXTOK % nc == 0
    row_own = rows_of_slots(frame_tokens, frame_sample, own, slots)
    row_sib = rows_of_slots(frame_tokens, frame_sample, sibling, slots)
    row_of = jnp.where(from_own, row_own, jnp.where(row_sib >= 0, row_sib + total_rows, -1))
    def cross(value, near, by):
        pairs = []
        for y in range(ny):
            for z in range(nz):
                for c in range(nc):
                    to = (y, (z + by) % nz) if (c == 0) == near else ((y + by) % ny, z)
                    pairs.append(((y * nz + z) * nc + c, (to[0] * nz + to[1]) * nc + c))
        return lax.ppermute(value, VDP, pairs)

    steps = (0, -1, 1, 2)
    line = jnp.concatenate([proj_weight] + [cross(proj_weight, True, d) for d in (1, -1, 2)])
    mine = lax.dynamic_slice_in_dim(line, ic * half, half, 1)
    theirs = shift(lax.dynamic_slice_in_dim(line, (1 - ic) * half, half, 1), CORE, 1)
    lines = list(tie(mine, theirs, activated))
    activated = lines[2]
    send_box = gather_spots(spots[:, :, None], columns, ny * nz, nc)
    right = shift(activated, X, 1)
    left = shift(tie(activated, send_box)[0], X, -1)
    plus = [cross(lines[0], False, 1), cross(lines[1], True, 1)]
    minus = [cross(lines[0], False, -1), cross(lines[1], True, -1)]
    everyone = jnp.concatenate(
        [
            activated,
            right,
            left,
            shift(tie(right, send_box)[0][: own_rows // 2], X, 1),
            shift(tie(left, send_box)[0][own_rows // 2 :], X, -1),
        ]
    )
    plus[0], plus[1], minus[0], minus[1], everyone = tie(*plus, *minus, everyone)
    middle = 2 * krows
    far = [
        (
            cross(plus[whose][:middle], whose == 1, 1),
            cross(minus[whose][middle:], whose == 1, -1),
        )
        for whose in range(nc)
    ]
    pieces, places = [], []
    for whose in range(nc):
        which = ic if whose == 0 else 1 - ic
        for piece, nears, away_by in (
            (lines[whose], steps, 0),
            (plus[whose], steps, -1),
            (minus[whose], steps, 1),
            (far[whose][0], steps[:2], 2),
            (far[whose][1], steps[2:], 2),
        ):
            pieces.append(piece)
            for near_by in nears:
                dy = jnp.where(which == 0, away_by, near_by)
                dz = jnp.where(which == 0, near_by, away_by)
                places.append((((iy + dy) % ny * nz + (iz + dz) % nz) * nc + which) * krows)
    places = jnp.stack(places).astype(jnp.int32)

    away_by = (row_of // own_rows - ix) % nx
    seat = jnp.where(away_by == nx - 1, 1, jnp.where(away_by == 0, 0, away_by + 1))
    act_row = jnp.where(
        row_of < 0, -1, row_of // total_rows * total_rows + seat * own_rows + row_of % own_rows
    )

    returned = lax.all_to_all(
        send_box.reshape(groups, nc * MAXTOK, half), VDP, split_axis=0, concat_axis=0, tiled=True
    )
    returned = tie(returned, *far[0], *far[1])[0]
    row_grad = unpick_rows(row_of[None, :], returned.reshape(n_slots, half), nc * total_rows)

    other = shift(everyone, CORE, 1)
    act_slots = pick_rows(act_row[:, None], everyone, other, hidden // 4)

    bias = lax.dynamic_slice_in_dim(proj_bias, ic * half, half, 0).astype(jnp.float32)[None, :]
    row_grad, act_slots = tie(row_grad, act_slots)
    kept_sum, away, weight = project_back(places, row_grad, pieces, krows, hidden)
    received = shift(away, CORE, 1).reshape(nx, own_rows, hidden)
    kept_sum = kept_sum.reshape(nx, own_rows, hidden)
    projected = project(act_slots, bias, weight, 0, 2, [])

    def part(d):
        here = (ix + d) % nx
        mine = lax.dynamic_index_in_dim(kept_sum, here, 0, keepdims=False)
        theirs = lax.dynamic_index_in_dim(received, here, 0, keepdims=False)
        return mine.astype(jnp.float32) + theirs.astype(jnp.float32)

    mid = hidden // 2
    far = part(2).astype(jnp.bfloat16)
    far, act_slots = tie(far, act_slots)
    projected = project(act_slots, bias, weight, 1, 2, [projected])
    incoming = lax.all_to_all(
        projected.reshape(groups, nc * MAXTOK, half), VDP, split_axis=0, concat_axis=0, tiled=True
    ).reshape(ny * nz, nc, nc * MAXTOK, half)

    far_right = shift(far[:, :mid], X, 1)
    far_left = shift(far[:, mid:], X, -1)
    to_right, to_left = part(1), part(-1)
    got_right_top = shift((to_right[:, :mid] + far_right.astype(jnp.float32)).astype(jnp.bfloat16), X, 1)
    got_right_end = shift(to_right[:, mid:].astype(jnp.bfloat16), X, 1)
    got_left_top = shift(to_left[:, :mid].astype(jnp.bfloat16), X, -1)
    got_left_end = shift((to_left[:, mid:] + far_left.astype(jnp.float32)).astype(jnp.bfloat16), X, -1)
    arrived = jnp.concatenate(
        [
            got_right_top.astype(jnp.float32) + got_left_top.astype(jnp.float32),
            got_right_end.astype(jnp.float32) + got_left_end.astype(jnp.float32),
        ],
        axis=1,
    )
    summed = part(0) + arrived
    slope = cdf + rows * jnp.exp(-0.5 * rows * rows) * 0.3989422804014327
    pre_grad = (summed * slope).astype(jnp.bfloat16)

    line = scatter_spots(spots[:, None, :], incoming, nx, span)
    placed = lax.all_to_all(line, X, split_axis=0, concat_axis=0, tiled=True)
    placed, pre_grad = tie(placed, pre_grad)
    return (join_columns(placed), pre_grad)


def solution(mesh):
    fine = Mesh(mesh.devices.reshape(4, 4, 2, 4), ALL)
    in_specs = (P(ALL, None), P(VDP, X), P(X), P(), P(), P(), P(ALL, None))
    out_specs = (P(ALL, None), P(ALL, None))
    return jax.shard_map(local, mesh=fine, in_specs=in_specs, out_specs=out_specs, check_vma=False)
```

```python
import jax
import jax.numpy as jnp
from jax import lax
from jax.experimental import pallas as pl
from jax.experimental.pallas import tpu as pltpu
from jax.sharding import Mesh, PartitionSpec as P

MAXTOK = 8
Y, Z, CORE, X = "y", "z", "core", "seq"
VDP = (Y, Z, CORE)
ALL = (Y, Z, CORE, X)


def normal_cdf(values):
    return 0.5 * (1.0 + jax.scipy.special.erf(values * 0.7071067811865476))


def shift(value, axis, by):
    size = lax.axis_size(axis)
    return lax.ppermute(value, axis, [(i, (i + by) % size) for i in range(size)])


def tie(*values):
    return lax.optimization_barrier(values)


def rows_of_slots(frame_tokens, frame_sample, group, slots):
    tokens = lax.dynamic_slice_in_dim(frame_tokens, group, 1, 0)
    sample = lax.dynamic_slice_in_dim(frame_sample, group, 1, 0)
    frame_ids = jnp.arange(frame_tokens.shape[1], dtype=jnp.int32)
    before = frame_ids[None, :] < frame_ids[:, None]
    starts = jnp.sum(jnp.where(before, tokens, 0), axis=1)[None, :]
    hit = sample == slots // MAXTOK
    step = slots[:, 0] % MAXTOK
    start = jnp.sum(jnp.where(hit, starts, 0), axis=1)
    length = jnp.sum(jnp.where(hit, tokens, 0), axis=1)
    return jnp.where(step < length, start + step, -1)


def spots_of_slots(frame_tokens, frame_sample, clip_offset, own_seq, group_of_slot, step):
    length = jnp.sum(jnp.where(frame_sample == own_seq, frame_tokens, 0), axis=1)[None, :]
    seq_ids = jnp.arange(clip_offset.shape[1], dtype=jnp.int32)
    offset = jnp.sum(jnp.where(seq_ids[None, :] == own_seq, clip_offset, 0), axis=1)[None, :]
    group_ids = jnp.arange(frame_tokens.shape[0], dtype=jnp.int32)
    owner = group_of_slot[:, None] == group_ids[None, :]
    slot_length = jnp.sum(jnp.where(owner, length, 0), axis=1)
    slot_offset = jnp.sum(jnp.where(owner, offset, 0), axis=1)
    return jnp.where(step < slot_length, slot_offset + step, -1)


VMEM_LIMIT = 48 * 1024 * 1024


def kernel_params():
    return pltpu.CompilerParams(vmem_limit_bytes=VMEM_LIMIT)


def cost(flops, moved):
    return pl.CostEstimate(flops=int(flops), bytes_accessed=int(moved), transcendentals=0)


def split_columns(table, parts):
    rows, total = table.shape
    width = total // parts

    def body(in_ref, out_ref):
        out_ref[0] = in_ref[...]

    return pl.pallas_call(
        body,
        grid=(parts,),
        in_specs=[pl.BlockSpec((rows, width), lambda j: (0, j))],
        out_specs=pl.BlockSpec((1, rows, width), lambda j: (j, 0, 0)),
        out_shape=jax.ShapeDtypeStruct((parts, rows, width), table.dtype),
        compiler_params=kernel_params(),
        cost_estimate=cost(0, 4 * rows * total),
        name="split_columns",
    )(table)


def join_columns(table):
    parts, rows, width = table.shape

    def body(in_ref, out_ref):
        out_ref[...] = in_ref[0]

    return pl.pallas_call(
        body,
        grid=(parts,),
        in_specs=[pl.BlockSpec((1, rows, width), lambda j: (j, 0, 0))],
        out_specs=pl.BlockSpec((rows, width), lambda j: (0, j)),
        out_shape=jax.ShapeDtypeStruct((rows, parts * width), table.dtype),
        compiler_params=kernel_params(),
        cost_estimate=cost(0, 4 * rows * parts * width),
        name="join_columns",
    )(table)


def hot_rows(index, count):
    ids = lax.broadcasted_iota(jnp.int32, (index.shape[0], count), 1)
    return jnp.where(index == ids, 1.0, 0.0).astype(jnp.bfloat16)


def hot_columns(index, count):
    ids = lax.broadcasted_iota(jnp.int32, (count, index.shape[1]), 0)
    return jnp.where(index == ids, 1.0, 0.0).astype(jnp.bfloat16)


def exact(selector, table):
    return jnp.dot(selector, table, preferred_element_type=jnp.float32).astype(jnp.bfloat16)


def gather_spots(spots, columns, chips, cores):
    n = spots.shape[1]
    parts, span, slab = columns.shape
    half = slab // cores
    per = n // chips

    def body(spot_ref, table_ref, out_ref):
        table = table_ref[...].reshape(parts * span, half)
        picked = exact(hot_rows(spot_ref[0], parts * span), table)
        out_ref[...] = picked.reshape(chips, 1, per, half)

    return pl.pallas_call(
        body,
        grid=(cores,),
        in_specs=[
            pl.BlockSpec((1, n, 1), lambda c: (c, 0, 0)),
            pl.BlockSpec((parts, span, half), lambda c: (0, 0, c)),
        ],
        out_specs=pl.BlockSpec((chips, 1, per, half), lambda c: (0, c, 0, 0)),
        out_shape=jax.ShapeDtypeStruct((chips, cores, per, half), columns.dtype),
        compiler_params=kernel_params(),
        cost_estimate=cost(2 * n * parts * span * slab, 4 * parts * span * slab),
        name="gather_spots",
    )(spots, columns)


def scatter_spots(spots, incoming, parts, span):
    chips, cores, per, half = incoming.shape
    n = chips * per

    def body(spot_ref, table_ref, out_ref):
        table = table_ref[...].reshape(n, half)
        placed = exact(hot_columns(spot_ref[0], parts * span), table)
        out_ref[...] = placed.reshape(parts, span, half)

    return pl.pallas_call(
        body,
        grid=(cores,),
        in_specs=[
            pl.BlockSpec((1, 1, n), lambda c: (c, 0, 0)),
            pl.BlockSpec((chips, 1, per, half), lambda c: (0, c, 0, 0)),
        ],
        out_specs=pl.BlockSpec((parts, span, half), lambda c: (0, 0, c)),
        out_shape=jax.ShapeDtypeStruct((parts, span, cores * half), incoming.dtype),
        compiler_params=kernel_params(),
        cost_estimate=cost(2 * n * parts * span * cores * half, 4 * parts * span * cores * half),
        name="scatter_spots",
    )(spots, incoming)


def pick_rows(index, own, other, width):
    n = index.shape[0]
    rows, total = own.shape

    def body(index_ref, own_ref, other_ref, out_ref):
        selector = hot_rows(index_ref[...], 2 * rows)
        picked = jnp.dot(selector[:, :rows], own_ref[...], preferred_element_type=jnp.float32)
        picked += jnp.dot(selector[:, rows:], other_ref[...], preferred_element_type=jnp.float32)
        out_ref[...] = picked.astype(jnp.bfloat16)

    return pl.pallas_call(
        body,
        grid=(total // width,),
        in_specs=[
            pl.BlockSpec((n, 1), lambda j: (0, 0)),
            pl.BlockSpec((rows, width), lambda j: (0, j)),
            pl.BlockSpec((rows, width), lambda j: (0, j)),
        ],
        out_specs=pl.BlockSpec((n, width), lambda j: (0, j)),
        out_shape=jax.ShapeDtypeStruct((n, total), own.dtype),
        compiler_params=kernel_params(),
        cost_estimate=cost(4 * n * rows * total, 8 * rows * total),
        name="pick_rows",
    )(index, own, other)


def unpick_rows(index, table, rows):
    n, width = table.shape

    def body(index_ref, table_ref, out_ref):
        out_ref[...] = exact(hot_columns(index_ref[...], rows), table_ref[...])

    return pl.pallas_call(
        body,
        out_shape=jax.ShapeDtypeStruct((rows, width), table.dtype),
        compiler_params=kernel_params(),
        cost_estimate=cost(2 * n * rows * width, 4 * rows * width),
        name="unpick_rows",
    )(index, table)


def project_back(places, grad, pieces, block, hidden):
    n, half = grad.shape
    tile = 1024
    count = len(pieces)
    blocks = [(p, b * block) for p in range(count) for b in range(pieces[p].shape[0] // block)]

    def body(*refs):
        place_ref, grad_ref = refs[:2]
        piece_refs = refs[2 : 2 + count]
        kept_ref, away_ref, weight_ref, held, arrive, leave = refs[2 + count :]
        copies = []
        for i, (p, start) in enumerate(blocks):
            first = pl.multiple_of(place_ref[i], block)
            copies.append(
                pltpu.make_async_copy(
                    piece_refs[p].at[pl.ds(start, block)],
                    held.at[pl.ds(first, block)],
                    arrive.at[i],
                )
            )
        for copy in copies:
            copy.start()
        for copy in copies:
            copy.wait()
        onward = pltpu.make_async_copy(held, weight_ref, leave)
        onward.start()

        @pl.loop(0, hidden // tile)
        def _(j):
            span = pl.ds(pl.multiple_of(j * tile, tile), tile)
            product = lax.dot_general(
                grad_ref[...],
                held[span, :],
                (((1,), (1,)), ((), ())),
                preferred_element_type=jnp.float32,
            )
            kept_ref[:, span] = product[: n // 2].astype(jnp.bfloat16)
            away_ref[:, span] = product[n // 2 :].astype(jnp.bfloat16)

        onward.wait()

    vmem = pl.BlockSpec(memory_space=pltpu.VMEM)
    anywhere = pl.BlockSpec(memory_space=pl.ANY)
    return pl.pallas_call(
        body,
        in_specs=[pl.BlockSpec(memory_space=pltpu.SMEM), vmem] + [anywhere] * count,
        out_specs=[vmem, vmem, anywhere],
        out_shape=[
            jax.ShapeDtypeStruct((n // 2, hidden), jnp.bfloat16),
            jax.ShapeDtypeStruct((n // 2, hidden), jnp.bfloat16),
            jax.ShapeDtypeStruct((hidden, half), jnp.bfloat16),
        ],
        scratch_shapes=[
            pltpu.VMEM((hidden, half), jnp.bfloat16),
            pltpu.SemaphoreType.DMA((len(blocks),)),
            pltpu.SemaphoreType.DMA,
        ],
        compiler_params=kernel_params(),
        cost_estimate=cost(2 * n * hidden * half, 6 * hidden * half),
        name="project_back",
    )(places, grad, *pieces)


def project(act, bias, weight):
    n, k = act.shape
    half = weight.shape[1]
    tile = 512
    last = k // tile - 1

    def body(act_ref, bias_ref, weight_ref, out_ref, total):
        j = pl.program_id(0)
        product = jnp.dot(act_ref[...], weight_ref[...], preferred_element_type=jnp.float32)

        @pl.when(j == 0)
        def _():
            total[...] = product

        @pl.when(j > 0)
        def _():
            total[...] += product

        @pl.when(j == last)
        def _():
            out_ref[...] = (total[...] + bias_ref[...]).astype(jnp.bfloat16)

    return pl.pallas_call(
        body,
        grid=(k // tile,),
        in_specs=[
            pl.BlockSpec((n, tile), lambda j: (0, j)),
            pl.BlockSpec((1, half), lambda j: (0, 0)),
            pl.BlockSpec((tile, half), lambda j: (j, 0)),
        ],
        out_specs=pl.BlockSpec((n, half), lambda j: (0, 0)),
        out_shape=jax.ShapeDtypeStruct((n, half), jnp.bfloat16),
        scratch_shapes=[pltpu.VMEM((n, half), jnp.float32)],
        compiler_params=kernel_params(),
        cost_estimate=cost(2 * n * k * half, 2 * k * half),
        name="project",
    )(act, bias, weight)


def local(pre_act, proj_weight, proj_bias, frame_tokens, frame_sample, clip_offset, embed_grad):
    ny, nz, nc, nx = (lax.axis_size(a) for a in ALL)
    iy, iz, ic, ix = (lax.axis_index(a) for a in ALL)
    chip = iy * nz + iz
    own = chip * nc + ic
    sibling = chip * nc + 1 - ic
    groups = ny * nz * nc
    own_rows, hidden = pre_act.shape
    total_rows = own_rows * nx
    span = embed_grad.shape[0]
    seq_len = span * nx
    krows, slab = proj_weight.shape
    half = slab // nc
    slot_total = groups * MAXTOK

    rows = pre_act.astype(jnp.float32)
    cdf = normal_cdf(rows)
    activated = (rows * cdf).astype(jnp.bfloat16)
    columns = lax.all_to_all(
        split_columns(embed_grad, nx), X, split_axis=0, concat_axis=0, tiled=True
    )

    step = jnp.arange(slot_total, dtype=jnp.int32) % MAXTOK
    pair = jnp.arange(slot_total, dtype=jnp.int32) // (nc * MAXTOK)
    member = jnp.arange(slot_total, dtype=jnp.int32) // MAXTOK % nc
    spots = jnp.stack(
        [
            spots_of_slots(
                frame_tokens, frame_sample, clip_offset, own, pair * nc + (member if c == 0 else 1 - member), step
            )
            for c in range(nc)
        ]
    )
    n_slots = nc * slot_total
    ids = lax.broadcasted_iota(jnp.int32, (n_slots, groups), 0)
    slots = ids // (nc * MAXTOK) * MAXTOK + ids % MAXTOK
    from_own = ids[:, 0] // MAXTOK % nc == 0
    row_own = rows_of_slots(frame_tokens, frame_sample, own, slots)
    row_sib = rows_of_slots(frame_tokens, frame_sample, sibling, slots)
    row_of = jnp.where(from_own, row_own, jnp.where(row_sib >= 0, row_sib + total_rows, -1))
    def cross(value, near, by):
        pairs = []
        for y in range(ny):
            for z in range(nz):
                for c in range(nc):
                    to = (y, (z + by) % nz) if (c == 0) == near else ((y + by) % ny, z)
                    pairs.append(((y * nz + z) * nc + c, (to[0] * nz + to[1]) * nc + c))
        return lax.ppermute(value, VDP, pairs)

    steps = (0, -1, 1, 2)
    line = jnp.concatenate([proj_weight] + [cross(proj_weight, True, d) for d in (1, -1, 2)])
    mine = lax.dynamic_slice_in_dim(line, ic * half, half, 1)
    theirs = shift(lax.dynamic_slice_in_dim(line, (1 - ic) * half, half, 1), CORE, 1)
    right, left = shift(activated, X, 1), shift(activated, X, -1)
    lines = list(tie(mine, theirs, right, left))
    right, left = lines[2:]
    plus = [cross(lines[0], False, 1), cross(lines[1], True, 1)]
    minus = [cross(lines[0], False, -1), cross(lines[1], True, -1)]
    plus[0], plus[1], minus[0], minus[1], columns = tie(*plus, *minus, columns)
    middle = 2 * krows
    far = [
        (
            cross(plus[whose][:middle], whose == 1, 1),
            cross(minus[whose][middle:], whose == 1, -1),
        )
        for whose in range(nc)
    ]
    pieces, places = [], []
    for whose in range(nc):
        which = ic if whose == 0 else 1 - ic
        for piece, nears, away_by in (
            (lines[whose], steps, 0),
            (plus[whose], steps, -1),
            (minus[whose], steps, 1),
            (far[whose][0], steps[:2], 2),
            (far[whose][1], steps[2:], 2),
        ):
            pieces.append(piece)
            for near_by in nears:
                dy = jnp.where(which == 0, away_by, near_by)
                dz = jnp.where(which == 0, near_by, away_by)
                places.append((((iy + dy) % ny * nz + (iz + dz) % nz) * nc + which) * krows)
    places = jnp.stack(places).astype(jnp.int32)

    send_box = gather_spots(spots[:, :, None], columns, ny * nz, nc)
    everyone = jnp.concatenate(
        [
            activated,
            right,
            left,
            shift(right[: own_rows // 2], X, 1),
            shift(left[own_rows // 2 :], X, -1),
        ]
    )
    away_by = (row_of // own_rows - ix) % nx
    seat = jnp.where(away_by == nx - 1, 1, jnp.where(away_by == 0, 0, away_by + 1))
    act_row = jnp.where(
        row_of < 0, -1, row_of // total_rows * total_rows + seat * own_rows + row_of % own_rows
    )

    returned = lax.all_to_all(
        send_box.reshape(groups, nc * MAXTOK, half), VDP, split_axis=0, concat_axis=0, tiled=True
    )

    other = shift(everyone, CORE, 1)
    act_slots = pick_rows(act_row[:, None], everyone, other, hidden // 4)

    bias = lax.dynamic_slice_in_dim(proj_bias, ic * half, half, 0).astype(jnp.float32)[None, :]
    returned, act_slots = tie(returned, act_slots, *far[0], *far[1])[:2]
    row_grad = unpick_rows(row_of[None, :], returned.reshape(n_slots, half), nc * total_rows)
    kept_sum, away, weight = project_back(places, row_grad, pieces, krows, hidden)
    received = shift(away, CORE, 1).reshape(nx, own_rows, hidden)
    kept_sum = kept_sum.reshape(nx, own_rows, hidden)
    projected = project(act_slots, bias, weight)
    incoming = lax.all_to_all(
        projected.reshape(groups, nc * MAXTOK, half), VDP, split_axis=0, concat_axis=0, tiled=True
    ).reshape(ny * nz, nc, nc * MAXTOK, half)

    def part(d):
        here = (ix + d) % nx
        mine = lax.dynamic_index_in_dim(kept_sum, here, 0, keepdims=False)
        theirs = lax.dynamic_index_in_dim(received, here, 0, keepdims=False)
        return mine.astype(jnp.float32) + theirs.astype(jnp.float32)

    mid = hidden // 2
    far = part(2).astype(jnp.bfloat16)
    far_right = shift(far[:, :mid], X, 1)
    far_left = shift(far[:, mid:], X, -1)
    to_right, to_left = part(1), part(-1)
    got_right_top = shift((to_right[:, :mid] + far_right.astype(jnp.float32)).astype(jnp.bfloat16), X, 1)
    got_right_end = shift(to_right[:, mid:].astype(jnp.bfloat16), X, 1)
    got_left_top = shift(to_left[:, :mid].astype(jnp.bfloat16), X, -1)
    got_left_end = shift((to_left[:, mid:] + far_left.astype(jnp.float32)).astype(jnp.bfloat16), X, -1)
    arrived = jnp.concatenate(
        [
            got_right_top.astype(jnp.float32) + got_left_top.astype(jnp.float32),
            got_right_end.astype(jnp.float32) + got_left_end.astype(jnp.float32),
        ],
        axis=1,
    )
    summed = part(0) + arrived
    slope = cdf + rows * jnp.exp(-0.5 * rows * rows) * 0.3989422804014327
    pre_grad = (summed * slope).astype(jnp.bfloat16)

    line = scatter_spots(spots[:, None, :], incoming, nx, span)
    placed = lax.all_to_all(line, X, split_axis=0, concat_axis=0, tiled=True)
    placed, pre_grad = tie(placed, pre_grad)
    return (join_columns(placed), pre_grad)


def solution(mesh):
    fine = Mesh(mesh.devices.reshape(4, 4, 2, 4), ALL)
    in_specs = (P(ALL, None), P(VDP, X), P(X), P(), P(), P(), P(ALL, None))
    out_specs = (P(ALL, None), P(ALL, None))
    return jax.shard_map(local, mesh=fine, in_specs=in_specs, out_specs=out_specs, check_vma=False)
```

```python
import jax
import jax.numpy as jnp
from jax import lax
from jax.experimental import pallas as pl
from jax.experimental.pallas import tpu as pltpu
from jax.sharding import Mesh, PartitionSpec as P

MAXTOK = 8
Y, Z, CORE, X = "y", "z", "core", "seq"
VDP = (Y, Z, CORE)
ALL = (Y, Z, CORE, X)


def normal_cdf(values):
    return 0.5 * (1.0 + jax.scipy.special.erf(values * 0.7071067811865476))


def shift(value, axis, by):
    size = lax.axis_size(axis)
    return lax.ppermute(value, axis, [(i, (i + by) % size) for i in range(size)])


def tie(*values):
    return lax.optimization_barrier(values)


def rows_of_slots(frame_tokens, frame_sample, group, slots):
    tokens = lax.dynamic_slice_in_dim(frame_tokens, group, 1, 0)
    sample = lax.dynamic_slice_in_dim(frame_sample, group, 1, 0)
    frame_ids = jnp.arange(frame_tokens.shape[1], dtype=jnp.int32)
    before = frame_ids[None, :] < frame_ids[:, None]
    starts = jnp.sum(jnp.where(before, tokens, 0), axis=1)[None, :]
    hit = sample == slots // MAXTOK
    step = slots[:, 0] % MAXTOK
    start = jnp.sum(jnp.where(hit, starts, 0), axis=1)
    length = jnp.sum(jnp.where(hit, tokens, 0), axis=1)
    return jnp.where(step < length, start + step, -1)


def spots_of_slots(frame_tokens, frame_sample, clip_offset, own_seq, group_of_slot, step):
    length = jnp.sum(jnp.where(frame_sample == own_seq, frame_tokens, 0), axis=1)[None, :]
    seq_ids = jnp.arange(clip_offset.shape[1], dtype=jnp.int32)
    offset = jnp.sum(jnp.where(seq_ids[None, :] == own_seq, clip_offset, 0), axis=1)[None, :]
    group_ids = jnp.arange(frame_tokens.shape[0], dtype=jnp.int32)
    owner = group_of_slot[:, None] == group_ids[None, :]
    slot_length = jnp.sum(jnp.where(owner, length, 0), axis=1)
    slot_offset = jnp.sum(jnp.where(owner, offset, 0), axis=1)
    return jnp.where(step < slot_length, slot_offset + step, -1)


VMEM_LIMIT = 48 * 1024 * 1024


def kernel_params():
    return pltpu.CompilerParams(vmem_limit_bytes=VMEM_LIMIT)


def cost(flops, moved):
    return pl.CostEstimate(flops=int(flops), bytes_accessed=int(moved), transcendentals=0)


def split_columns(table, parts):
    rows, total = table.shape
    width = total // parts

    def body(in_ref, out_ref):
        out_ref[0] = in_ref[...]

    return pl.pallas_call(
        body,
        grid=(parts,),
        in_specs=[pl.BlockSpec((rows, width), lambda j: (0, j))],
        out_specs=pl.BlockSpec((1, rows, width), lambda j: (j, 0, 0)),
        out_shape=jax.ShapeDtypeStruct((parts, rows, width), table.dtype),
        compiler_params=kernel_params(),
        cost_estimate=cost(0, 4 * rows * total),
        name="split_columns",
    )(table)


def join_columns(table):
    parts, rows, width = table.shape

    def body(in_ref, out_ref):
        out_ref[...] = in_ref[0]

    return pl.pallas_call(
        body,
        grid=(parts,),
        in_specs=[pl.BlockSpec((1, rows, width), lambda j: (j, 0, 0))],
        out_specs=pl.BlockSpec((rows, width), lambda j: (0, j)),
        out_shape=jax.ShapeDtypeStruct((rows, parts * width), table.dtype),
        compiler_params=kernel_params(),
        cost_estimate=cost(0, 4 * rows * parts * width),
        name="join_columns",
    )(table)


def hot_rows(index, count):
    ids = lax.broadcasted_iota(jnp.int32, (index.shape[0], count), 1)
    return jnp.where(index == ids, 1.0, 0.0).astype(jnp.bfloat16)


def hot_columns(index, count):
    ids = lax.broadcasted_iota(jnp.int32, (count, index.shape[1]), 0)
    return jnp.where(index == ids, 1.0, 0.0).astype(jnp.bfloat16)


def exact(selector, table):
    return jnp.dot(selector, table, preferred_element_type=jnp.float32).astype(jnp.bfloat16)


def gather_spots(spots, columns, chips, cores):
    n = spots.shape[1]
    parts, span, slab = columns.shape
    half = slab // cores
    per = n // chips

    def body(spot_ref, table_ref, out_ref):
        table = table_ref[...].reshape(parts * span, half)
        picked = exact(hot_rows(spot_ref[0], parts * span), table)
        out_ref[...] = picked.reshape(chips, 1, per, half)

    return pl.pallas_call(
        body,
        grid=(cores,),
        in_specs=[
            pl.BlockSpec((1, n, 1), lambda c: (c, 0, 0)),
            pl.BlockSpec((parts, span, half), lambda c: (0, 0, c)),
        ],
        out_specs=pl.BlockSpec((chips, 1, per, half), lambda c: (0, c, 0, 0)),
        out_shape=jax.ShapeDtypeStruct((chips, cores, per, half), columns.dtype),
        compiler_params=kernel_params(),
        cost_estimate=cost(2 * n * parts * span * slab, 4 * parts * span * slab),
        name="gather_spots",
    )(spots, columns)


def scatter_spots(spots, incoming, parts, span):
    chips, cores, per, half = incoming.shape
    n = chips * per

    def body(spot_ref, table_ref, out_ref):
        table = table_ref[...].reshape(n, half)
        placed = exact(hot_columns(spot_ref[0], parts * span), table)
        out_ref[...] = placed.reshape(parts, span, half)

    return pl.pallas_call(
        body,
        grid=(cores,),
        in_specs=[
            pl.BlockSpec((1, 1, n), lambda c: (c, 0, 0)),
            pl.BlockSpec((chips, 1, per, half), lambda c: (0, c, 0, 0)),
        ],
        out_specs=pl.BlockSpec((parts, span, half), lambda c: (0, 0, c)),
        out_shape=jax.ShapeDtypeStruct((parts, span, cores * half), incoming.dtype),
        compiler_params=kernel_params(),
        cost_estimate=cost(2 * n * parts * span * cores * half, 4 * parts * span * cores * half),
        name="scatter_spots",
    )(spots, incoming)


def pick_rows(index, own, other, width):
    n = index.shape[0]
    rows, total = own.shape

    def body(index_ref, own_ref, other_ref, out_ref):
        selector = hot_rows(index_ref[...], 2 * rows)
        picked = jnp.dot(selector[:, :rows], own_ref[...], preferred_element_type=jnp.float32)
        picked += jnp.dot(selector[:, rows:], other_ref[...], preferred_element_type=jnp.float32)
        out_ref[...] = picked.astype(jnp.bfloat16)

    return pl.pallas_call(
        body,
        grid=(total // width,),
        in_specs=[
            pl.BlockSpec((n, 1), lambda j: (0, 0)),
            pl.BlockSpec((rows, width), lambda j: (0, j)),
            pl.BlockSpec((rows, width), lambda j: (0, j)),
        ],
        out_specs=pl.BlockSpec((n, width), lambda j: (0, j)),
        out_shape=jax.ShapeDtypeStruct((n, total), own.dtype),
        compiler_params=kernel_params(),
        cost_estimate=cost(4 * n * rows * total, 8 * rows * total),
        name="pick_rows",
    )(index, own, other)


def unpick_rows(index, table, rows):
    n, width = table.shape

    def body(index_ref, table_ref, out_ref):
        out_ref[...] = exact(hot_columns(index_ref[...], rows), table_ref[...])

    return pl.pallas_call(
        body,
        out_shape=jax.ShapeDtypeStruct((rows, width), table.dtype),
        compiler_params=kernel_params(),
        cost_estimate=cost(2 * n * rows * width, 4 * rows * width),
        name="unpick_rows",
    )(index, table)


def project_back(places, grad, pieces, block, hidden):
    n, half = grad.shape
    tile = 1024
    count = len(pieces)
    blocks = [(p, b * block) for p in range(count) for b in range(pieces[p].shape[0] // block)]

    def body(*refs):
        place_ref, grad_ref = refs[:2]
        piece_refs = refs[2 : 2 + count]
        kept_ref, away_ref, weight_ref, held, arrive, leave = refs[2 + count :]
        copies = []
        for i, (p, start) in enumerate(blocks):
            first = pl.multiple_of(place_ref[i], block)
            copies.append(
                pltpu.make_async_copy(
                    piece_refs[p].at[pl.ds(start, block)],
                    held.at[pl.ds(first, block)],
                    arrive.at[i],
                )
            )
        for copy in copies:
            copy.start()
        for copy in copies:
            copy.wait()
        onward = pltpu.make_async_copy(held, weight_ref, leave)
        onward.start()

        @pl.loop(0, hidden // tile)
        def _(j):
            span = pl.ds(pl.multiple_of(j * tile, tile), tile)
            product = lax.dot_general(
                grad_ref[...],
                held[span, :],
                (((1,), (1,)), ((), ())),
                preferred_element_type=jnp.float32,
            )
            kept_ref[:, span] = product[: n // 2].astype(jnp.bfloat16)
            away_ref[:, span] = product[n // 2 :].astype(jnp.bfloat16)

        onward.wait()

    vmem = pl.BlockSpec(memory_space=pltpu.VMEM)
    anywhere = pl.BlockSpec(memory_space=pl.ANY)
    return pl.pallas_call(
        body,
        in_specs=[pl.BlockSpec(memory_space=pltpu.SMEM), vmem] + [anywhere] * count,
        out_specs=[vmem, vmem, anywhere],
        out_shape=[
            jax.ShapeDtypeStruct((n // 2, hidden), jnp.bfloat16),
            jax.ShapeDtypeStruct((n // 2, hidden), jnp.bfloat16),
            jax.ShapeDtypeStruct((hidden, half), jnp.bfloat16),
        ],
        scratch_shapes=[
            pltpu.VMEM((hidden, half), jnp.bfloat16),
            pltpu.SemaphoreType.DMA((len(blocks),)),
            pltpu.SemaphoreType.DMA,
        ],
        compiler_params=kernel_params(),
        cost_estimate=cost(2 * n * hidden * half, 6 * hidden * half),
        name="project_back",
    )(places, grad, *pieces)


def project(act, bias, weight):
    n, k = act.shape
    half = weight.shape[1]
    tile = 512
    last = k // tile - 1

    def body(act_ref, bias_ref, weight_ref, out_ref, total):
        j = pl.program_id(0)
        product = jnp.dot(act_ref[...], weight_ref[...], preferred_element_type=jnp.float32)

        @pl.when(j == 0)
        def _():
            total[...] = product

        @pl.when(j > 0)
        def _():
            total[...] += product

        @pl.when(j == last)
        def _():
            out_ref[...] = (total[...] + bias_ref[...]).astype(jnp.bfloat16)

    return pl.pallas_call(
        body,
        grid=(k // tile,),
        in_specs=[
            pl.BlockSpec((n, tile), lambda j: (0, j)),
            pl.BlockSpec((1, half), lambda j: (0, 0)),
            pl.BlockSpec((tile, half), lambda j: (j, 0)),
        ],
        out_specs=pl.BlockSpec((n, half), lambda j: (0, 0)),
        out_shape=jax.ShapeDtypeStruct((n, half), jnp.bfloat16),
        scratch_shapes=[pltpu.VMEM((n, half), jnp.float32)],
        compiler_params=kernel_params(),
        cost_estimate=cost(2 * n * k * half, 2 * k * half),
        name="project",
    )(act, bias, weight)


def local(pre_act, proj_weight, proj_bias, frame_tokens, frame_sample, clip_offset, embed_grad):
    ny, nz, nc, nx = (lax.axis_size(a) for a in ALL)
    iy, iz, ic, ix = (lax.axis_index(a) for a in ALL)
    chip = iy * nz + iz
    own = chip * nc + ic
    sibling = chip * nc + 1 - ic
    groups = ny * nz * nc
    own_rows, hidden = pre_act.shape
    total_rows = own_rows * nx
    span = embed_grad.shape[0]
    seq_len = span * nx
    krows, slab = proj_weight.shape
    half = slab // nc
    slot_total = groups * MAXTOK

    rows = pre_act.astype(jnp.float32)
    cdf = normal_cdf(rows)
    activated = (rows * cdf).astype(jnp.bfloat16)
    columns = lax.all_to_all(
        split_columns(embed_grad, nx), X, split_axis=0, concat_axis=0, tiled=True
    )

    step = jnp.arange(slot_total, dtype=jnp.int32) % MAXTOK
    pair = jnp.arange(slot_total, dtype=jnp.int32) // (nc * MAXTOK)
    member = jnp.arange(slot_total, dtype=jnp.int32) // MAXTOK % nc
    spots = jnp.stack(
        [
            spots_of_slots(
                frame_tokens, frame_sample, clip_offset, own, pair * nc + (member if c == 0 else 1 - member), step
            )
            for c in range(nc)
        ]
    )
    n_slots = nc * slot_total
    ids = lax.broadcasted_iota(jnp.int32, (n_slots, groups), 0)
    slots = ids // (nc * MAXTOK) * MAXTOK + ids % MAXTOK
    from_own = ids[:, 0] // MAXTOK % nc == 0
    row_own = rows_of_slots(frame_tokens, frame_sample, own, slots)
    row_sib = rows_of_slots(frame_tokens, frame_sample, sibling, slots)
    row_of = jnp.where(from_own, row_own, jnp.where(row_sib >= 0, row_sib + total_rows, -1))
    def cross(value, near, by):
        pairs = []
        for y in range(ny):
            for z in range(nz):
                for c in range(nc):
                    to = (y, (z + by) % nz) if (c == 0) == near else ((y + by) % ny, z)
                    pairs.append(((y * nz + z) * nc + c, (to[0] * nz + to[1]) * nc + c))
        return lax.ppermute(value, VDP, pairs)

    steps = (0, -1, 1, 2)
    line = jnp.concatenate([proj_weight] + [cross(proj_weight, True, d) for d in (1, -1, 2)])
    mine = lax.dynamic_slice_in_dim(line, ic * half, half, 1)
    theirs = shift(lax.dynamic_slice_in_dim(line, (1 - ic) * half, half, 1), CORE, 1)
    lines = list(tie(mine, theirs, columns, activated))
    columns, activated = lines[2:]
    right, left = shift(activated, X, 1), shift(activated, X, -1)
    plus = [cross(lines[0], False, 1), cross(lines[1], True, 1)]
    minus = [cross(lines[0], False, -1), cross(lines[1], True, -1)]
    send_box = gather_spots(spots[:, :, None], columns, ny * nz, nc)
    everyone = jnp.concatenate(
        [
            activated,
            right,
            left,
            shift(tie(right, send_box)[0][: own_rows // 2], X, 1),
            shift(tie(left, send_box)[0][own_rows // 2 :], X, -1),
        ]
    )
    plus[0], plus[1], minus[0], minus[1], everyone = tie(*plus, *minus, everyone)
    middle = 2 * krows
    far = [
        (
            cross(plus[whose][:middle], whose == 1, 1),
            cross(minus[whose][middle:], whose == 1, -1),
        )
        for whose in range(nc)
    ]
    pieces, places = [], []
    for whose in range(nc):
        which = ic if whose == 0 else 1 - ic
        for piece, nears, away_by in (
            (lines[whose], steps, 0),
            (plus[whose], steps, -1),
            (minus[whose], steps, 1),
            (far[whose][0], steps[:2], 2),
            (far[whose][1], steps[2:], 2),
        ):
            pieces.append(piece)
            for near_by in nears:
                dy = jnp.where(which == 0, away_by, near_by)
                dz = jnp.where(which == 0, near_by, away_by)
                places.append((((iy + dy) % ny * nz + (iz + dz) % nz) * nc + which) * krows)
    places = jnp.stack(places).astype(jnp.int32)

    away_by = (row_of // own_rows - ix) % nx
    seat = jnp.where(away_by == nx - 1, 1, jnp.where(away_by == 0, 0, away_by + 1))
    act_row = jnp.where(
        row_of < 0, -1, row_of // total_rows * total_rows + seat * own_rows + row_of % own_rows
    )

    returned = lax.all_to_all(
        send_box.reshape(groups, nc * MAXTOK, half), VDP, split_axis=0, concat_axis=0, tiled=True
    )

    other = shift(everyone, CORE, 1)
    act_slots = pick_rows(act_row[:, None], everyone, other, hidden // 4)

    bias = lax.dynamic_slice_in_dim(proj_bias, ic * half, half, 0).astype(jnp.float32)[None, :]
    returned, act_slots = tie(returned, act_slots, *far[0], *far[1])[:2]
    row_grad = unpick_rows(row_of[None, :], returned.reshape(n_slots, half), nc * total_rows)
    kept_sum, away, weight = project_back(places, row_grad, pieces, krows, hidden)
    received = shift(away, CORE, 1).reshape(nx, own_rows, hidden)
    kept_sum = kept_sum.reshape(nx, own_rows, hidden)
    projected = project(act_slots, bias, weight)
    incoming = lax.all_to_all(
        projected.reshape(groups, nc * MAXTOK, half), VDP, split_axis=0, concat_axis=0, tiled=True
    ).reshape(ny * nz, nc, nc * MAXTOK, half)

    def part(d):
        here = (ix + d) % nx
        mine = lax.dynamic_index_in_dim(kept_sum, here, 0, keepdims=False)
        theirs = lax.dynamic_index_in_dim(received, here, 0, keepdims=False)
        return mine.astype(jnp.float32) + theirs.astype(jnp.float32)

    mid = hidden // 2
    far = part(2).astype(jnp.bfloat16)
    far_right = shift(far[:, :mid], X, 1)
    far_left = shift(far[:, mid:], X, -1)
    to_right, to_left = part(1), part(-1)
    got_right_top = shift((to_right[:, :mid] + far_right.astype(jnp.float32)).astype(jnp.bfloat16), X, 1)
    got_right_end = shift(to_right[:, mid:].astype(jnp.bfloat16), X, 1)
    got_left_top = shift(to_left[:, :mid].astype(jnp.bfloat16), X, -1)
    got_left_end = shift((to_left[:, mid:] + far_left.astype(jnp.float32)).astype(jnp.bfloat16), X, -1)
    arrived = jnp.concatenate(
        [
            got_right_top.astype(jnp.float32) + got_left_top.astype(jnp.float32),
            got_right_end.astype(jnp.float32) + got_left_end.astype(jnp.float32),
        ],
        axis=1,
    )
    summed = part(0) + arrived
    slope = cdf + rows * jnp.exp(-0.5 * rows * rows) * 0.3989422804014327
    pre_grad = (summed * slope).astype(jnp.bfloat16)

    line = scatter_spots(spots[:, None, :], incoming, nx, span)
    placed = lax.all_to_all(line, X, split_axis=0, concat_axis=0, tiled=True)
    placed, pre_grad = tie(placed, pre_grad)
    return (join_columns(placed), pre_grad)


def solution(mesh):
    fine = Mesh(mesh.devices.reshape(4, 4, 2, 4), ALL)
    in_specs = (P(ALL, None), P(VDP, X), P(X), P(), P(), P(), P(ALL, None))
    out_specs = (P(ALL, None), P(ALL, None))
    return jax.shard_map(local, mesh=fine, in_specs=in_specs, out_specs=out_specs, check_vma=False)
```
